128 devices in a mesh: seq: 32 (over x, z, core), head: 4 (over y).
Axes of the slice: x: 4, y: 4, z: 4, core: 2. Of those that a mesh axis runs over, the one named last changes fastest.
Arguments:
- queries: bfloat16 [16384, 4096], P(('head', 'seq')), may hold values from -6 to 6
- keys: bfloat16 [16384, 4096], P(('head', 'seq')), may hold values from -6 to 6
- values: bfloat16 [16384, 4096], P(('head', 'seq')), may hold values from -6 to 6
- key_blocks: int32 [32, 128, 48], P('seq'), may hold values from 0 to 127, as said below
- key_count: int32 [32, 128], P('seq'), may hold values from 1 to 48, as said below
Outputs:
- attended: bfloat16 [16384, 4096], P(('head', 'seq'))
The draws below stay inside these ranges and needn't reach their ends.
Inputs may be any that keep to these rules, and one draw needn't show every extreme that they name: `key_blocks`: entries of one list are distinct; the first entry is the query block itself. `key_count`: heads differ in how many key blocks their query blocks use.
All inputs are finite; a program needn't handle non-finite values.
Results may differ from the reference program's by a relative error of at most 0.0046.
Values may be sent and summed in bfloat16 or wider, within the bound.
No kernel may reach another device: no remote copies, remote signals or barrier semaphores. Data moves between devices by JAX's collectives and lax.ppermute only.
A program may use at most 128 MiB of HBM per device.

```python
import jax
import jax.numpy as jnp
from jax import lax

HDIM = 128
BLOCK = 128
HEADS = 32
TOKENS = 16384
NB = 128
KEYS_MOST = 48


def draw_queries(key, part):
    key = jax.random.fold_in(key, 3)
    base = jnp.clip(jax.random.normal(key, (TOKENS, HEADS * HDIM), jnp.float32), -6.0, 6.0)
    return base.astype(jnp.bfloat16)


def draw_keys(key, part):
    key = jax.random.fold_in(key, 5)
    base = jnp.clip(jax.random.normal(key, (TOKENS, HEADS * HDIM), jnp.float32), -6.0, 6.0)
    return base.astype(jnp.bfloat16)


def draw_key_blocks(key, part):
    key = jax.random.fold_in(key, 11)
    noise = jax.random.randint(key, (HEADS, NB, NB), 0, 1 << 16, dtype=jnp.int32)
    column = jnp.arange(NB, dtype=jnp.int32)
    query_row = column[:, None]
    scores = noise * NB + column[None, None, :]
    near = jnp.abs(column[None, :] - query_row) <= 2
    scores = scores + jnp.where(near, 1 << 22, 0)[None]
    scores = scores + jnp.where(column[None, :] == query_row, 1 << 25, 0)[None]
    picked = lax.top_k(scores, KEYS_MOST)[1]
    return picked.astype(jnp.int32)


def draw_key_count(key, part):
    key = jax.random.fold_in(key, 23)
    first, second, third, fourth = jax.random.split(key, 4)
    heads = jnp.arange(HEADS, dtype=jnp.int32)
    head_most = jax.random.randint(first, (HEADS,), KEYS_MOST // 4, KEYS_MOST + 1, dtype=jnp.int32)
    busiest = jax.random.randint(second, (), 0, HEADS, dtype=jnp.int32)
    head_most = jnp.where(heads == busiest, KEYS_MOST, head_most)
    counts = jax.random.randint(third, (HEADS, NB), 1, head_most[:, None] + 1, dtype=jnp.int32)
    top_row = jax.random.randint(fourth, (HEADS,), 0, NB, dtype=jnp.int32)
    blocks = jnp.arange(NB, dtype=jnp.int32)
    counts = jnp.where(blocks[None, :] == top_row[:, None], head_most[:, None], counts)
    return counts.astype(jnp.int32)


def levels(stream_key, extent, cuts, smallest, high):
    gain = 1.0
    for position, blocks in cuts:
        draws = jax.random.uniform(jax.random.fold_in(jax.random.fold_in(stream_key, 6), position), (blocks,), jnp.float32, smallest / len(cuts), high / len(cuts))
        gain = gain * jnp.repeat(jnp.exp(draws), extent[position] // blocks).reshape((-1,) + (1,) * (len(extent) - 1 - position))
    return gain


def centred(own_key, shape, scale, most, pieces=(), held_as=jnp.bfloat16):
    values = jax.random.normal(own_key, shape, jnp.float32) * scale
    if len(pieces) > 0:
        values = levels(own_key, shape, pieces, -0.22, 0.18) * values
    return jnp.clip(values, min=-most, max=most).astype(held_as)


def setup_inputs(seed: int = 0) -> dict:
    key_of = jax.random.split(jax.random.key(seed), 6)
    return {
        "queries": draw_queries(jax.random.fold_in(key_of[5], 71), 0),
        "keys": draw_keys(jax.random.fold_in(key_of[5], 71), 0),
        "values": centred(key_of[2], (TOKENS, HEADS * HDIM), 1.0, 6.0, ((0, 128),)),
        "key_blocks": draw_key_blocks(jax.random.fold_in(key_of[5], 71), 0),
        "key_count": draw_key_count(jax.random.fold_in(key_of[5], 71), 0),
    }


def one_head(args):
    q_head, k_head, v_head, lists, counts = args
    k_blocks = k_head.reshape(NB, BLOCK, HDIM)
    v_blocks = v_head.reshape(NB, BLOCK, HDIM)
    q_blocks = q_head.reshape(NB, BLOCK, HDIM)
    scale = 1.0 / (HDIM ** 0.5)

    def one_block(inner):
        q_block, listed, count = inner
        key_rows = k_blocks[listed].reshape(KEYS_MOST * BLOCK, HDIM)
        val_rows = v_blocks[listed].reshape(KEYS_MOST * BLOCK, HDIM)
        score = jnp.dot(q_block, key_rows.T, preferred_element_type=jnp.float32) * scale
        valid = (jnp.arange(KEYS_MOST * BLOCK, dtype=jnp.int32) // BLOCK) < count
        score = jnp.where(valid[None, :], score, -jnp.inf)
        top = jnp.max(score, axis=1, keepdims=True)
        weight = jnp.exp(score - top)
        total = jnp.sum(weight, axis=1, keepdims=True)
        weight_b = weight.astype(jnp.bfloat16)
        summed = jnp.dot(weight_b, val_rows, preferred_element_type=jnp.float32)
        return (summed / total).astype(jnp.bfloat16)

    result = lax.map(one_block, (q_blocks, lists, counts))
    return result.reshape(TOKENS, HDIM)


def reference(queries, keys, values, key_blocks, key_count):
    q_heads = jnp.transpose(queries.reshape(TOKENS, HEADS, HDIM), (1, 0, 2))
    k_heads = jnp.transpose(keys.reshape(TOKENS, HEADS, HDIM), (1, 0, 2))
    v_heads = jnp.transpose(values.reshape(TOKENS, HEADS, HDIM), (1, 0, 2))
    result = lax.map(one_head, (q_heads, k_heads, v_heads, key_blocks, key_count))
    return jnp.transpose(result, (1, 0, 2)).reshape(TOKENS, HEADS * HDIM)
```

```python
import functools

import jax
import jax.numpy as jnp
from jax import lax
from jax.experimental import pallas as pl
from jax.experimental.pallas import tpu as pltpu
from jax.sharding import PartitionSpec as P

BLOCK = 128
HDIM = 128
LOG2E = 1.4426950408889634


def pack_kernel(q_ref, k_ref, v_ref, qo_ref, ko_ref, vo_ref):
    for h in range(qo_ref.shape[0]):
        cols = slice(h * HDIM, (h + 1) * HDIM)
        qo_ref[h] = q_ref[:, cols]
        ko_ref[h] = k_ref[:, cols]
        vo_ref[h] = v_ref[:, cols].T


def pack(queries, keys, values):
    tok, width = queries.shape
    heads = width // HDIM
    per = 8
    flat = pl.BlockSpec((tok, per * HDIM), lambda i: (0, i))
    blocks = pl.BlockSpec((per, tok, HDIM), lambda i: (i, 0, 0))
    out = jax.ShapeDtypeStruct((heads, tok, HDIM), queries.dtype)
    return pl.pallas_call(
        pack_kernel,
        grid=(heads // per,),
        in_specs=[flat] * 3,
        out_specs=[blocks] * 3,
        out_shape=[out] * 3,
    )(queries, keys, values)


def unpack_kernel(x_ref, o_ref):
    for h in range(x_ref.shape[0]):
        o_ref[:, h * HDIM : (h + 1) * HDIM] = x_ref[h]


def unpack(x):
    heads, tok, hdim = x.shape
    per = 8
    return pl.pallas_call(
        unpack_kernel,
        grid=(heads // per,),
        in_specs=[pl.BlockSpec((per, tok, hdim), lambda i: (i, 0, 0))],
        out_specs=pl.BlockSpec((tok, per * hdim), lambda i: (0, i)),
        out_shape=jax.ShapeDtypeStruct((tok, heads * hdim), x.dtype),
    )(x)


def attention_kernel(group, most, lists, counts, q_ref, k_ref, vt_ref, o_ref):
    factor = LOG2E / HDIM**0.5

    def query_block(b, _):
        q = q_ref[b]
        count = counts[b]

        def chunk(c, carry):
            top, total, acc = carry
            scores, places, active = [], [], []
            for g in range(group):
                j = c * group + g
                place = lists[b * most + jnp.minimum(j, count - 1)]
                places.append(place)
                active.append(j < count)
                scores.append(
                    lax.dot_general(
                        k_ref[place], q, (((1,), (1,)), ((), ())), preferred_element_type=jnp.float32
                    )
                )
            largest = functools.reduce(jnp.maximum, scores)
            new_top = jnp.maximum(top, jnp.max(largest, axis=0, keepdims=True) * factor)
            shrink = jnp.exp2(top - new_top)
            total = total * shrink
            acc = acc * shrink
            for g in range(group):
                base = jnp.where(active[g], new_top, jnp.inf)
                weight = jnp.exp2(scores[g] * factor - base)
                total = total + weight.reshape(BLOCK // 8, 8, BLOCK).sum(axis=0)
                acc = acc + lax.dot_general(
                    vt_ref[places[g]],
                    weight.astype(jnp.bfloat16),
                    (((1,), (0,)), ((), ())),
                    preferred_element_type=jnp.float32,
                )
            return new_top, total, acc

        first = (
            jnp.full((1, BLOCK), -jnp.inf, jnp.float32),
            jnp.zeros((8, BLOCK), jnp.float32),
            jnp.zeros((HDIM, BLOCK), jnp.float32),
        )
        _, total, acc = lax.fori_loop(0, (count + group - 1) // group, chunk, first)
        out = acc / jnp.sum(total, axis=0, keepdims=True)
        o_ref[b] = out.T.astype(jnp.bfloat16)
        return 0

    lax.fori_loop(0, q_ref.shape[0], query_block, 0)


def attention(lists, counts, q, k, vt, group=8):
    whole = lambda a: pl.BlockSpec(a.shape, lambda i, *_: (0, 0, 0))
    return pl.pallas_call(
        functools.partial(attention_kernel, group, lists.shape[1]),
        grid_spec=pltpu.PrefetchScalarGridSpec(
            num_scalar_prefetch=2,
            grid=(1,),
            in_specs=[whole(q), whole(k), whole(vt)],
            out_specs=whole(q),
        ),
        out_shape=jax.ShapeDtypeStruct(q.shape, jnp.bfloat16),
        compiler_params=pltpu.CompilerParams(vmem_limit_bytes=48 << 20),
    )(lists.reshape(-1), counts, q, k, vt)


def local(queries, keys, values, key_blocks, key_count):
    swap = lambda a: lax.all_to_all(a, "seq", split_axis=0, concat_axis=0, tiled=True)
    gather = lambda a: lax.all_gather(a, "head", axis=0, tiled=True)
    q, k, vt = pack(queries, keys, values)
    k_all = gather(swap(k))
    vt_all = gather(swap(vt))
    q_mine = swap(q)
    q_count = q_mine.shape[0]
    first_block = lax.axis_index("head") * q_count
    lists = lax.dynamic_slice_in_dim(key_blocks[0], first_block, q_count, 0)
    counts = lax.dynamic_slice_in_dim(key_count[0], first_block, q_count, 0)
    result = attention(lists, counts, q_mine, k_all, vt_all)
    return unpack(swap(result))


def solution(mesh):
    placed = (
        P(("head", "seq"), None),
        P(("head", "seq"), None),
        P(("head", "seq"), None),
        P("seq", None, None),
        P("seq", None),
    )
    return jax.shard_map(
        local, mesh=mesh, in_specs=placed, out_specs=P(("head", "seq"), None), check_vma=False
    )
```

```python
import functools

import jax
import jax.numpy as jnp
from jax import lax
from jax.experimental import pallas as pl
from jax.experimental.pallas import tpu as pltpu
from jax.sharding import PartitionSpec as P

BLOCK = 128
HDIM = 128
LOG2E = 1.4426950408889634
FACTOR = LOG2E / HDIM**0.5
GROUP = 8
PLACES = 16
VMEM = 48 << 20


def pack_kv_kernel(k_ref, v_ref, o_ref):
    for h in range(o_ref.shape[0] * o_ref.shape[1]):
        cols = slice(h * HDIM, (h + 1) * HDIM)
        o_ref[h % 2, h // 2, 0] = k_ref[:, cols]
        o_ref[h % 2, h // 2, 1] = v_ref[:, cols].T


def pack_q_kernel(q_ref, o_ref):
    for h in range(o_ref.shape[0] * o_ref.shape[1]):
        o_ref[h % 2, h // 2] = q_ref[:, h * HDIM : (h + 1) * HDIM]


def unpack_kernel(x_ref, o_ref):
    for h in range(x_ref.shape[0] * x_ref.shape[1]):
        o_ref[:, h * HDIM : (h + 1) * HDIM] = x_ref[h % 2, h // 2]


STEP = 4
FLAT = pl.BlockSpec((BLOCK, 2 * STEP * HDIM), lambda i: (0, i))
PACKED = pl.BlockSpec((2, STEP, BLOCK, HDIM), lambda i: (0, i, 0, 0))


def pack_kv(keys, values):
    return pl.pallas_call(
        pack_kv_kernel,
        grid=(PLACES // STEP,),
        in_specs=[FLAT, FLAT],
        out_specs=pl.BlockSpec((2, STEP, 2, BLOCK, HDIM), lambda i: (0, i, 0, 0, 0)),
        out_shape=jax.ShapeDtypeStruct((2, PLACES, 2, BLOCK, HDIM), keys.dtype),
    )(keys, values)


def pack_q(queries):
    return pl.pallas_call(
        pack_q_kernel,
        grid=(PLACES // STEP,),
        in_specs=[FLAT],
        out_specs=PACKED,
        out_shape=jax.ShapeDtypeStruct((2, PLACES, BLOCK, HDIM), queries.dtype),
    )(queries)


def unpack(x):
    return pl.pallas_call(
        unpack_kernel,
        grid=(PLACES // STEP,),
        in_specs=[PACKED],
        out_specs=FLAT,
        out_shape=jax.ShapeDtypeStruct((BLOCK, 2 * PLACES * HDIM), x.dtype),
    )(x)


def attention_kernel(
    first, last, chunks, lists, counts, q_hbm, own_hbm, other_hbm, *rest
):
    rest = list(rest)
    if not first:
        acc_in, top_in, total_in = (rest.pop(0) for _ in range(3))
    if last:
        o_ref = rest.pop(0)
        acc_ref, top_ref, total_ref = rest[6:9]
    else:
        acc_ref, top_ref, total_ref = (rest.pop(0) for _ in range(3))
    s0, s1, p0, p1, q_ref, kv_ref = rest[:6]
    sems = rest[-1]
    nq = q_hbm.shape[0]
    half = own_hbm.shape[0]
    most = lists.shape[0] // (nq + 1)

    copies = [
        (q_hbm, q_ref),
        (own_hbm, kv_ref.at[pl.ds(0, half)]),
        (other_hbm, kv_ref.at[pl.ds(half, half)]),
    ]
    if not first:
        copies += [(acc_in, acc_ref), (top_in, top_ref), (total_in, total_ref)]
    copies = [
        pltpu.make_async_copy(src, dst, sems.at[i]) for i, (src, dst) in enumerate(copies)
    ]
    for copy in copies:
        copy.start()
    if first:
        acc_ref[...] = jnp.zeros_like(acc_ref)
        top_ref[...] = jnp.full_like(top_ref, -jnp.inf)
        total_ref[...] = jnp.zeros_like(total_ref)
    for copy in copies:
        copy.wait()

    def where(t):
        code = chunks[t + 1]
        return code // 8, code % 8

    def places(b, c):
        end = jnp.maximum(counts[b] - 1, 0)
        return [lists[b * most + jnp.minimum(c * GROUP + g, end)] for g in range(GROUP)]

    def scores(b, chosen, dst):
        rows = jnp.concatenate([kv_ref[i, 0] for i in chosen], axis=0)
        q = q_ref[jnp.minimum(b, nq - 1)]
        s = lax.dot_general(rows, q, (((1,), (1,)), ((), ())), preferred_element_type=jnp.float32)
        dst[...] = s
        return jnp.max(s.reshape(GROUP * BLOCK // 8, 8, BLOCK), axis=0)

    def weights(b, c, largest, src, dst, top, total):
        count = counts[b]
        top = jnp.where(c == 0, top_ref[b], top)
        total = jnp.where(c == 0, total_ref[b], total)
        new_top = jnp.maximum(top, jnp.max(largest, axis=0, keepdims=True) * FACTOR)
        shrink = jnp.exp2(top - new_top)
        total = total * shrink
        for g in range(GROUP):
            rows = slice(g * BLOCK, (g + 1) * BLOCK)
            base = jnp.where(c * GROUP + g < count, new_top, jnp.inf)
            weight = jnp.exp2(src[rows, :] * FACTOR - base)
            total = total + jnp.sum(weight.reshape(BLOCK // 8, 8, BLOCK), axis=0)
            dst[rows, :] = weight.astype(jnp.bfloat16)
        top_ref[b] = new_top
        total_ref[b] = total
        return new_top, total, shrink

    def weighted(b, chosen, shrink, src):
        cols = jnp.concatenate([kv_ref[i, 1] for i in chosen], axis=1)
        acc_ref[b] = acc_ref[b] * shrink + jnp.dot(
            cols, src[...], preferred_element_type=jnp.float32
        )

    steps = chunks[0]
    score_bufs, weight_bufs = (s0, s1), (p0, p1)
    b0, c0 = where(0)
    places0 = places(b0, c0)
    largest0 = scores(b0, places0, s0)
    b1, c1 = where(1)
    places1 = places(b1, c1)
    largest1 = scores(b1, places1, s1)
    top, total, shrink0 = weights(
        b0,
        c0,
        largest0,
        s0,
        p0,
        jnp.full((1, BLOCK), -jnp.inf, jnp.float32),
        jnp.zeros((8, BLOCK), jnp.float32),
    )

    def body(i, carry):
        b0, shrink0, b1, c1, largest1, top, total = carry[:7]
        places0, places1 = list(carry[7 : 7 + GROUP]), list(carry[7 + GROUP :])
        for u in range(2):
            b2, c2 = where(2 * i + u + 2)
            places2 = places(b2, c2)
            largest2 = scores(b2, places2, score_bufs[u])
            top, total, shrink1 = weights(
                b1, c1, largest1, score_bufs[1 - u], weight_bufs[1 - u], top, total
            )
            weighted(b0, places0, shrink0, weight_bufs[u])
            b0, shrink0, places0 = b1, shrink1, places1
            b1, c1, largest1, places1 = b2, c2, largest2, places2
        return (b0, shrink0, b1, c1, largest1, top, total, *places0, *places1)

    lax.fori_loop(
        0,
        (steps + 1) // 2,
        body,
        (b0, shrink0, b1, c1, largest1, top, total, *places0, *places1),
    )

    if last:

        def finish(b, _):
            out = acc_ref[b] / jnp.sum(total_ref[b], axis=0, keepdims=True)
            o_ref[b] = out.T.astype(jnp.bfloat16)
            return 0

        lax.fori_loop(0, nq, finish, 0, unroll=4)


def attention(tables, q, own, other, state, last):
    chunks, lists, counts = tables
    nq = q.shape[0]
    first = state is None
    hbm = pl.BlockSpec(memory_space=pl.ANY)
    shapes = [(nq + 1, HDIM, BLOCK), (nq + 1, 1, BLOCK), (nq + 1, 8, BLOCK)]
    whole = lambda s: pl.BlockSpec(s, lambda i, *_: (0, 0, 0))
    scratch = [
        pltpu.VMEM((GROUP * BLOCK, BLOCK), jnp.float32),
        pltpu.VMEM((GROUP * BLOCK, BLOCK), jnp.float32),
        pltpu.VMEM((GROUP * BLOCK, BLOCK), jnp.bfloat16),
        pltpu.VMEM((GROUP * BLOCK, BLOCK), jnp.bfloat16),
        pltpu.VMEM(q.shape, q.dtype),
        pltpu.VMEM((2 * own.shape[0],) + own.shape[1:], own.dtype),
    ]
    if last:
        scratch += [pltpu.VMEM(s, jnp.float32) for s in shapes]
        out_shape = jax.ShapeDtypeStruct(q.shape, jnp.bfloat16)
        out_specs = whole(q.shape)
    else:
        out_shape = [jax.ShapeDtypeStruct(s, jnp.float32) for s in shapes]
        out_specs = [whole(s) for s in shapes]
    scratch += [pltpu.SemaphoreType.DMA((6,))]
    args = [q, own, other] + ([] if first else list(state))
    return pl.pallas_call(
        functools.partial(attention_kernel, first, last),
        grid_spec=pltpu.PrefetchScalarGridSpec(
            num_scalar_prefetch=3,
            grid=(1,),
            in_specs=[hbm] * len(args),
            out_specs=out_specs,
            scratch_shapes=scratch,
        ),
        out_shape=out_shape,
        compiler_params=pltpu.CompilerParams(vmem_limit_bytes=VMEM),
        cost_estimate=pl.CostEstimate(
            flops=20_000_000_000, bytes_accessed=16 << 20, transcendentals=0
        ),
    )(chunks, lists, counts, *args)


def make_tables(match, place):
    nq, most = match.shape
    at = jnp.arange(most, dtype=jnp.int32)
    before = (at[:, None] < at[None, :])[None] & match[:, :, None]
    pos = jnp.sum(before.astype(jnp.int32), axis=1)
    hit = (pos[:, :, None] == at[None, None, :]) & match[:, :, None]
    lists = jnp.sum(jnp.where(hit, place[:, :, None], 0), axis=1)
    counts = jnp.sum(match.astype(jnp.int32), axis=1)
    steps = (counts + GROUP - 1) // GROUP
    row = jnp.arange(nq, dtype=jnp.int32)
    ends = jnp.sum(jnp.where(row[:, None] <= row[None, :], steps[:, None], 0), axis=0)
    t = jnp.arange(nq * ((most + GROUP - 1) // GROUP) + 3, dtype=jnp.int32)
    b = jnp.sum((t[:, None] >= ends[None, :]).astype(jnp.int32), axis=1)
    start = jnp.sum(jnp.where(row[None, :] < b[:, None], steps[None, :], 0), axis=1)
    c = jnp.where(b < nq, t - start, 0)
    chunks = jnp.concatenate([ends[-1:], b * 8 + c])
    lists = jnp.pad(lists, ((0, 1), (0, 0))).reshape(-1)
    return chunks, lists, jnp.pad(counts, (0, 1))


def local(queries, keys, values, key_blocks, key_count):
    seq_count, head_count = lax.axis_size("seq"), lax.axis_size("head")
    y = lax.axis_index("head")
    core = lax.axis_index("seq") % 2

    index = lambda place, c, yy: (place * 2 + c) * head_count + yy
    groups = [
        [index(place, c, yy) for yy in ys for place in range(PLACES)]
        for c in range(2)
        for ys in ((0, 3), (1, 2))
    ]
    swap = lambda a: lax.all_to_all(
        a, ("seq", "head"), 0, 0, axis_index_groups=groups, tiled=True
    )
    to_core = lambda a: lax.ppermute(a, "seq", [(i, i ^ 1) for i in range(seq_count)])
    to_pair = lambda a: lax.ppermute(a, "head", [(i, i ^ 1) for i in range(head_count)])

    odd = (y >= 2).astype(jnp.int32)
    mine = jnp.concatenate([key_blocks[0], key_count[0][:, None]], axis=1)
    mine = jnp.where(core == odd, mine, to_core(mine))
    outer = (y == 0) | (y == 3)
    mine = mine.reshape(head_count, PLACES, 2, -1)
    mine = lax.dynamic_index_in_dim(mine, core, 2, keepdims=False)
    mine = jnp.where(outer, mine[0::3], mine[1:3]).reshape(2 * PLACES, -1)
    blocks, count = mine[:, :-1], mine[:, -1]
    active = jnp.arange(blocks.shape[1], dtype=jnp.int32)[None, :] < count[:, None]
    block_y = blocks // 32
    block_core = (blocks % 2) ^ core
    block_place = (blocks // 2) % PLACES
    near = ((block_y == 0) | (block_y == 3)) == outer
    second = block_y // 2
    near_tables = make_tables(
        active & near, (block_core * 2 + second) * PLACES + block_place
    )
    far_place = block_core * PLACES + block_place
    far_tables = [make_tables(active & ~near & (second == i), far_place) for i in range(2)]

    kv = swap(pack_kv(keys, values).reshape(2 * PLACES, 2, BLOCK, HDIM))
    kv_far = [to_pair(kv[i * PLACES : (i + 1) * PLACES]) for i in range(2)]
    q = swap(pack_q(queries).reshape(2 * PLACES, BLOCK, HDIM))
    state = attention(near_tables, q, kv, to_core(kv), None, False)
    state, far = lax.optimization_barrier((state, kv_far[0]))
    state = attention(far_tables[0], q, far, to_core(far), state, False)
    state, far = lax.optimization_barrier((state, kv_far[1]))
    out = attention(far_tables[1], q, far, to_core(far), state, True)
    return unpack(swap(out).reshape(2, PLACES, BLOCK, HDIM))


def solution(mesh):
    placed = (
        P(("head", "seq"), None),
        P(("head", "seq"), None),
        P(("head", "seq"), None),
        P("seq", None, None),
        P("seq", None),
    )
    return jax.shard_map(
        local, mesh=mesh, in_specs=placed, out_specs=P(("head", "seq"), None), check_vma=False
    )
```

```python
import functools

import jax
import jax.numpy as jnp
from jax import lax
from jax.experimental import pallas as pl
from jax.experimental.pallas import tpu as pltpu
from jax.sharding import PartitionSpec as P

BLOCK = 128
HDIM = 128
LOG2E = 1.4426950408889634
FACTOR = LOG2E / HDIM**0.5
GROUP = 8
PLACES = 16
VMEM = 48 << 20


def pack_kv_kernel(k_ref, v_ref, o_ref):
    for h in range(o_ref.shape[0] * o_ref.shape[1]):
        cols = slice(h * HDIM, (h + 1) * HDIM)
        o_ref[h % 2, h // 2, 0] = k_ref[:, cols]
        o_ref[h % 2, h // 2, 1] = v_ref[:, cols].T


def pack_q_kernel(q_ref, o_ref):
    for h in range(o_ref.shape[0] * o_ref.shape[1]):
        o_ref[h % 2, h // 2] = q_ref[:, h * HDIM : (h + 1) * HDIM]


def unpack_kernel(x_ref, o_ref):
    for h in range(x_ref.shape[0] * x_ref.shape[1]):
        o_ref[:, h * HDIM : (h + 1) * HDIM] = x_ref[h % 2, h // 2]


STEP = 4
CUT = 12
FLAT = pl.BlockSpec((BLOCK, 2 * STEP * HDIM), lambda i: (0, i))
PACKED = pl.BlockSpec((2, STEP, BLOCK, HDIM), lambda i: (0, i, 0, 0))


def pack_kv(keys, values):
    return pl.pallas_call(
        pack_kv_kernel,
        grid=(PLACES // STEP,),
        in_specs=[FLAT, FLAT],
        out_specs=pl.BlockSpec((2, STEP, 2, BLOCK, HDIM), lambda i: (0, i, 0, 0, 0)),
        out_shape=jax.ShapeDtypeStruct((2, PLACES, 2, BLOCK, HDIM), keys.dtype),
    )(keys, values)


def pack_q(queries):
    return pl.pallas_call(
        pack_q_kernel,
        grid=(PLACES // STEP,),
        in_specs=[FLAT],
        out_specs=PACKED,
        out_shape=jax.ShapeDtypeStruct((2, PLACES, BLOCK, HDIM), queries.dtype),
    )(queries)


def unpack(x):
    return pl.pallas_call(
        unpack_kernel,
        grid=(PLACES // STEP,),
        in_specs=[PACKED],
        out_specs=FLAT,
        out_shape=jax.ShapeDtypeStruct((BLOCK, 2 * PLACES * HDIM), x.dtype),
    )(x)


def attention_kernel(
    first, last, chunks, lists, counts, q_hbm, own_hbm, other_hbm, *rest
):
    rest = list(rest)
    if not first:
        acc_in, top_in, total_in = (rest.pop(0) for _ in range(3))
    if last:
        o_ref = rest.pop(0)
        acc_ref, top_ref, total_ref = rest[6:9]
    else:
        acc_ref, top_ref, total_ref = (rest.pop(0) for _ in range(3))
    s0, s1, p0, p1, q_ref, kv_ref = rest[:6]
    sems = rest[-1]
    nq = q_hbm.shape[0]
    half = own_hbm.shape[0]
    most = lists.shape[0] // (nq + 1)

    copies = [
        (q_hbm, q_ref),
        (own_hbm, kv_ref.at[pl.ds(0, half)]),
        (other_hbm, kv_ref.at[pl.ds(half, half)]),
    ]
    if not first:
        copies += [(acc_in, acc_ref), (top_in, top_ref), (total_in, total_ref)]
    copies = [
        pltpu.make_async_copy(src, dst, sems.at[i]) for i, (src, dst) in enumerate(copies)
    ]
    for copy in copies:
        copy.start()
    if first:
        acc_ref[...] = jnp.zeros_like(acc_ref)
        top_ref[...] = jnp.full_like(top_ref, -jnp.inf)
        total_ref[...] = jnp.zeros_like(total_ref)
    for copy in copies:
        copy.wait()

    def where(t):
        code = chunks[t + 1]
        return code // 8, code % 8

    def places(b, c):
        end = jnp.maximum(counts[b] - 1, 0)
        return [lists[b * most + jnp.minimum(c * GROUP + g, end)] for g in range(GROUP)]

    def scores(b, chosen, dst):
        rows = jnp.concatenate([kv_ref[i, 0] for i in chosen], axis=0)
        q = q_ref[jnp.minimum(b, nq - 1)]
        s = lax.dot_general(rows, q, (((1,), (1,)), ((), ())), preferred_element_type=jnp.float32)
        dst[...] = s
        return jnp.max(s.reshape(GROUP * BLOCK // 8, 8, BLOCK), axis=0)

    def weights(b, c, largest, src, dst, top, total):
        count = counts[b]
        top = jnp.where(c == 0, top_ref[b], top)
        total = jnp.where(c == 0, total_ref[b], total)
        new_top = jnp.maximum(top, jnp.max(largest, axis=0, keepdims=True) * FACTOR)
        shrink = jnp.exp2(top - new_top)
        total = total * shrink
        for g in range(GROUP):
            rows = slice(g * BLOCK, (g + 1) * BLOCK)
            base = jnp.where(c * GROUP + g < count, new_top, jnp.inf)
            weight = jnp.exp2(src[rows, :] * FACTOR - base)
            total = total + jnp.sum(weight.reshape(BLOCK // 8, 8, BLOCK), axis=0)
            dst[rows, :] = weight.astype(jnp.bfloat16)
        top_ref[b] = new_top
        total_ref[b] = total
        return new_top, total, shrink

    def weighted(b, chosen, shrink, src):
        cols = jnp.concatenate([kv_ref[i, 1] for i in chosen], axis=1)
        acc_ref[b] = acc_ref[b] * shrink + jnp.dot(
            cols, src[...], preferred_element_type=jnp.float32
        )

    steps = chunks[0]
    score_bufs, weight_bufs = (s0, s1), (p0, p1)
    b0, c0 = where(0)
    places0 = places(b0, c0)
    largest0 = scores(b0, places0, s0)
    b1, c1 = where(1)
    places1 = places(b1, c1)
    largest1 = scores(b1, places1, s1)
    top, total, shrink0 = weights(
        b0,
        c0,
        largest0,
        s0,
        p0,
        jnp.full((1, BLOCK), -jnp.inf, jnp.float32),
        jnp.zeros((8, BLOCK), jnp.float32),
    )

    def body(i, carry):
        b0, shrink0, b1, c1, largest1, top, total = carry[:7]
        places0, places1 = list(carry[7 : 7 + GROUP]), list(carry[7 + GROUP :])
        for u in range(2):
            b2, c2 = where(2 * i + u + 2)
            places2 = places(b2, c2)
            largest2 = scores(b2, places2, score_bufs[u])
            top, total, shrink1 = weights(
                b1, c1, largest1, score_bufs[1 - u], weight_bufs[1 - u], top, total
            )
            weighted(b0, places0, shrink0, weight_bufs[u])
            b0, shrink0, places0 = b1, shrink1, places1
            b1, c1, largest1, places1 = b2, c2, largest2, places2
        return (b0, shrink0, b1, c1, largest1, top, total, *places0, *places1)

    lax.fori_loop(
        0,
        (steps + 1) // 2,
        body,
        (b0, shrink0, b1, c1, largest1, top, total, *places0, *places1),
    )

    if last:

        def finish(b, _):
            out = acc_ref[b] / jnp.sum(total_ref[b], axis=0, keepdims=True)
            o_ref[b] = out.T.astype(jnp.bfloat16)
            return 0

        lax.fori_loop(0, nq, finish, 0, unroll=4)


def attention(tables, q, own, other, state, last):
    chunks, lists, counts = tables
    nq = q.shape[0]
    first = state is None
    hbm = pl.BlockSpec(memory_space=pl.ANY)
    shapes = [(nq + 1, HDIM, BLOCK), (nq + 1, 1, BLOCK), (nq + 1, 8, BLOCK)]
    whole = lambda s: pl.BlockSpec(s, lambda i, *_: (0, 0, 0))
    scratch = [
        pltpu.VMEM((GROUP * BLOCK, BLOCK), jnp.float32),
        pltpu.VMEM((GROUP * BLOCK, BLOCK), jnp.float32),
        pltpu.VMEM((GROUP * BLOCK, BLOCK), jnp.bfloat16),
        pltpu.VMEM((GROUP * BLOCK, BLOCK), jnp.bfloat16),
        pltpu.VMEM(q.shape, q.dtype),
        pltpu.VMEM((2 * own.shape[0],) + own.shape[1:], own.dtype),
    ]
    if last:
        scratch += [pltpu.VMEM(s, jnp.float32) for s in shapes]
        out_shape = jax.ShapeDtypeStruct(q.shape, jnp.bfloat16)
        out_specs = whole(q.shape)
    else:
        out_shape = [jax.ShapeDtypeStruct(s, jnp.float32) for s in shapes]
        out_specs = [whole(s) for s in shapes]
    scratch += [pltpu.SemaphoreType.DMA((6,))]
    args = [q, own, other] + ([] if first else list(state))
    return pl.pallas_call(
        functools.partial(attention_kernel, first, last),
        grid_spec=pltpu.PrefetchScalarGridSpec(
            num_scalar_prefetch=3,
            grid=(1,),
            in_specs=[hbm] * len(args),
            out_specs=out_specs,
            scratch_shapes=scratch,
        ),
        out_shape=out_shape,
        compiler_params=pltpu.CompilerParams(vmem_limit_bytes=VMEM),
        cost_estimate=pl.CostEstimate(
            flops=1_000_000, bytes_accessed=1, transcendentals=0
        ),
    )(chunks, lists, counts, *args)


def make_tables(match, place):
    nq, most = match.shape
    at = jnp.arange(most, dtype=jnp.int32)
    before = (at[:, None] < at[None, :])[None] & match[:, :, None]
    pos = jnp.sum(before.astype(jnp.int32), axis=1)
    hit = (pos[:, :, None] == at[None, None, :]) & match[:, :, None]
    lists = jnp.sum(jnp.where(hit, place[:, :, None], 0), axis=1)
    counts = jnp.sum(match.astype(jnp.int32), axis=1)
    steps = (counts + GROUP - 1) // GROUP
    row = jnp.arange(nq, dtype=jnp.int32)
    ends = jnp.sum(jnp.where(row[:, None] <= row[None, :], steps[:, None], 0), axis=0)
    t = jnp.arange(nq * ((most + GROUP - 1) // GROUP) + 3, dtype=jnp.int32)
    b = jnp.sum((t[:, None] >= ends[None, :]).astype(jnp.int32), axis=1)
    start = jnp.sum(jnp.where(row[None, :] < b[:, None], steps[None, :], 0), axis=1)
    c = jnp.where(b < nq, t - start, 0)
    chunks = jnp.concatenate([ends[-1:], b * 8 + c])
    lists = jnp.pad(lists, ((0, 1), (0, 0))).reshape(-1)
    return chunks, lists, jnp.pad(counts, (0, 1))


def local(queries, keys, values, key_blocks, key_count):
    seq_count, head_count = lax.axis_size("seq"), lax.axis_size("head")
    y = lax.axis_index("head")
    core = lax.axis_index("seq") % 2

    index = lambda place, c, yy: (place * 2 + c) * head_count + yy
    groups = [
        [index(place, c, yy) for yy in ys for place in range(PLACES)]
        for c in range(2)
        for ys in ((0, 3), (1, 2))
    ]
    swap = lambda a: lax.all_to_all(
        a, ("seq", "head"), 0, 0, axis_index_groups=groups, tiled=True
    )
    to_core = lambda a: lax.ppermute(a, "seq", [(i, i ^ 1) for i in range(seq_count)])
    to_pair = lambda a: lax.ppermute(a, "head", [(i, i ^ 1) for i in range(head_count)])

    odd = (y >= 2).astype(jnp.int32)
    mine = jnp.concatenate([key_blocks[0], key_count[0][:, None]], axis=1)
    mine = jnp.where(core == odd, mine, to_core(mine))
    outer = (y == 0) | (y == 3)
    mine = mine.reshape(head_count, PLACES, 2, -1)
    mine = lax.dynamic_index_in_dim(mine, core, 2, keepdims=False)
    mine = jnp.where(outer, mine[0::3], mine[1:3]).reshape(2 * PLACES, -1)
    blocks, count = mine[:, :-1], mine[:, -1]
    active = jnp.arange(blocks.shape[1], dtype=jnp.int32)[None, :] < count[:, None]
    block_y = blocks // 32
    block_core = (blocks % 2) ^ core
    block_place = (blocks // 2) % PLACES
    near = ((block_y == 0) | (block_y == 3)) == outer
    block_at = (block_y // 2) * PLACES + block_place
    size = 2 * PLACES
    near_tables = make_tables(active & near, block_core * size + block_at)
    far_tables = [
        make_tables(active & ~near & (block_at < CUT), block_core * CUT + block_at),
        make_tables(
            active & ~near & (block_at >= CUT), block_core * (size - CUT) + block_at - CUT
        ),
    ]

    kv = swap(pack_kv(keys, values).reshape(2 * PLACES, 2, BLOCK, HDIM))
    kv_far = [to_pair(kv[:CUT]), to_pair(kv[CUT:])]
    q, near_tables, far_tables = lax.optimization_barrier(
        (pack_q(queries), near_tables, far_tables)
    )
    q = swap(q.reshape(2 * PLACES, BLOCK, HDIM))
    state = attention(near_tables, q, kv, to_core(kv), None, False)
    state, far = lax.optimization_barrier((state, kv_far[0]))
    state = attention(far_tables[0], q, far, to_core(far), state, False)
    state, far = lax.optimization_barrier((state, kv_far[1]))
    out = attention(far_tables[1], q, far, to_core(far), state, True)
    return unpack(swap(out).reshape(2, PLACES, BLOCK, HDIM))


def solution(mesh):
    placed = (
        P(("head", "seq"), None),
        P(("head", "seq"), None),
        P(("head", "seq"), None),
        P("seq", None, None),
        P("seq", None),
    )
    return jax.shard_map(
        local, mesh=mesh, in_specs=placed, out_specs=P(("head", "seq"), None), check_vma=False
    )
```

```python
import functools

import jax
import jax.numpy as jnp
from jax import lax
from jax.experimental import pallas as pl
from jax.experimental.pallas import tpu as pltpu
from jax.sharding import PartitionSpec as P

BLOCK = 128
HDIM = 128
LOG2E = 1.4426950408889634
FACTOR = LOG2E / HDIM**0.5
GROUP = 8
PLACES = 16
VMEM = 48 << 20


def pack_kv_kernel(k_ref, v_ref, o_ref):
    for h in range(o_ref.shape[0] * o_ref.shape[1]):
        cols = slice(h * HDIM, (h + 1) * HDIM)
        o_ref[h % 2, h // 2, 0] = k_ref[:, cols]
        o_ref[h % 2, h // 2, 1] = v_ref[:, cols].T


def pack_q_kernel(q_ref, o_ref):
    for h in range(o_ref.shape[0] * o_ref.shape[1]):
        o_ref[h % 2, h // 2] = q_ref[:, h * HDIM : (h + 1) * HDIM]


def unpack_kernel(x_ref, o_ref):
    for h in range(x_ref.shape[0] * x_ref.shape[1]):
        o_ref[:, h * HDIM : (h + 1) * HDIM] = x_ref[h % 2, h // 2]


STEP = 4
FLAT = pl.BlockSpec((BLOCK, 2 * STEP * HDIM), lambda i: (0, i))
PACKED = pl.BlockSpec((2, STEP, BLOCK, HDIM), lambda i: (0, i, 0, 0))


def pack_kv(keys, values):
    return pl.pallas_call(
        pack_kv_kernel,
        grid=(PLACES // STEP,),
        in_specs=[FLAT, FLAT],
        out_specs=pl.BlockSpec((2, STEP, 2, BLOCK, HDIM), lambda i: (0, i, 0, 0, 0)),
        out_shape=jax.ShapeDtypeStruct((2, PLACES, 2, BLOCK, HDIM), keys.dtype),
    )(keys, values)


def pack_q(queries):
    return pl.pallas_call(
        pack_q_kernel,
        grid=(PLACES // STEP,),
        in_specs=[FLAT],
        out_specs=PACKED,
        out_shape=jax.ShapeDtypeStruct((2, PLACES, BLOCK, HDIM), queries.dtype),
    )(queries)


def unpack(x):
    return pl.pallas_call(
        unpack_kernel,
        grid=(PLACES // STEP,),
        in_specs=[PACKED],
        out_specs=FLAT,
        out_shape=jax.ShapeDtypeStruct((BLOCK, 2 * PLACES * HDIM), x.dtype),
    )(x)


def attention_kernel(
    first, last, chunks, lists, counts, q_hbm, own_hbm, other_hbm, *rest
):
    rest = list(rest)
    if not first:
        acc_in, top_in, total_in = (rest.pop(0) for _ in range(3))
    if last:
        o_ref = rest.pop(0)
        acc_ref, top_ref, total_ref = rest[6:9]
    else:
        acc_ref, top_ref, total_ref = (rest.pop(0) for _ in range(3))
    s0, s1, p0, p1, q_ref, kv_ref = rest[:6]
    sems = rest[-1]
    nq = q_hbm.shape[0]
    half = own_hbm.shape[0]
    most = lists.shape[0] // (nq + 1)

    copies = [
        (q_hbm, q_ref),
        (own_hbm, kv_ref.at[pl.ds(0, half)]),
        (other_hbm, kv_ref.at[pl.ds(half, half)]),
    ]
    if not first:
        copies += [(acc_in, acc_ref), (top_in, top_ref), (total_in, total_ref)]
    copies = [
        pltpu.make_async_copy(src, dst, sems.at[i]) for i, (src, dst) in enumerate(copies)
    ]
    for copy in copies:
        copy.start()
    if first:
        acc_ref[...] = jnp.zeros_like(acc_ref)
        top_ref[...] = jnp.full_like(top_ref, -jnp.inf)
        total_ref[...] = jnp.zeros_like(total_ref)
    for copy in copies:
        copy.wait()

    def where(t):
        code = chunks[t + 1]
        return code // 8, code % 8

    def places(b, c):
        end = jnp.maximum(counts[b] - 1, 0)
        return [lists[b * most + jnp.minimum(c * GROUP + g, end)] for g in range(GROUP)]

    def scores(b, chosen, dst):
        rows = jnp.concatenate([kv_ref[i, 0] for i in chosen], axis=0)
        q = q_ref[jnp.minimum(b, nq - 1)]
        s = lax.dot_general(rows, q, (((1,), (1,)), ((), ())), preferred_element_type=jnp.float32)
        dst[...] = s
        return jnp.max(s.reshape(GROUP * BLOCK // 8, 8, BLOCK), axis=0)

    def weights(b, c, largest, src, dst, top, total):
        count = counts[b]
        top = jnp.where(c == 0, top_ref[b], top)
        total = jnp.where(c == 0, total_ref[b], total)
        new_top = jnp.maximum(top, jnp.max(largest, axis=0, keepdims=True) * FACTOR)
        shrink = jnp.exp2(top - new_top)
        total = total * shrink
        for g in range(GROUP):
            rows = slice(g * BLOCK, (g + 1) * BLOCK)
            base = jnp.where(c * GROUP + g < count, new_top, jnp.inf)
            weight = jnp.exp2(src[rows, :] * FACTOR - base)
            total = total + jnp.sum(weight.reshape(BLOCK // 8, 8, BLOCK), axis=0)
            dst[rows, :] = weight.astype(jnp.bfloat16)
        top_ref[b] = new_top
        total_ref[b] = total
        return new_top, total, shrink

    def weighted(b, chosen, shrink, src):
        cols = jnp.concatenate([kv_ref[i, 1] for i in chosen], axis=1)
        acc_ref[b] = acc_ref[b] * shrink + jnp.dot(
            cols, src[...], preferred_element_type=jnp.float32
        )

    steps = chunks[0]
    score_bufs, weight_bufs = (s0, s1), (p0, p1)
    b0, c0 = where(0)
    places0 = places(b0, c0)
    largest0 = scores(b0, places0, s0)
    b1, c1 = where(1)
    places1 = places(b1, c1)
    largest1 = scores(b1, places1, s1)
    top, total, shrink0 = weights(
        b0,
        c0,
        largest0,
        s0,
        p0,
        jnp.full((1, BLOCK), -jnp.inf, jnp.float32),
        jnp.zeros((8, BLOCK), jnp.float32),
    )

    def body(i, carry):
        b0, shrink0, b1, c1, largest1, top, total = carry[:7]
        places0, places1 = list(carry[7 : 7 + GROUP]), list(carry[7 + GROUP :])
        for u in range(4):
            b2, c2 = where(4 * i + u + 2)
            places2 = places(b2, c2)
            largest2 = scores(b2, places2, score_bufs[u % 2])
            top, total, shrink1 = weights(
                b1, c1, largest1, score_bufs[1 - u % 2], weight_bufs[1 - u % 2], top, total
            )
            weighted(b0, places0, shrink0, weight_bufs[u % 2])
            b0, shrink0, places0 = b1, shrink1, places1
            b1, c1, largest1, places1 = b2, c2, largest2, places2
        return (b0, shrink0, b1, c1, largest1, top, total, *places0, *places1)

    lax.fori_loop(
        0,
        (steps + 3) // 4,
        body,
        (b0, shrink0, b1, c1, largest1, top, total, *places0, *places1),
    )

    if last:

        def finish(b, _):
            out = acc_ref[b] / jnp.sum(total_ref[b], axis=0, keepdims=True)
            o_ref[b] = out.T.astype(jnp.bfloat16)
            return 0

        lax.fori_loop(0, nq, finish, 0, unroll=4)


def attention(tables, q, own, other, state, last):
    chunks, lists, counts = tables
    nq = q.shape[0]
    first = state is None
    hbm = pl.BlockSpec(memory_space=pl.ANY)
    shapes = [(nq + 1, HDIM, BLOCK), (nq + 1, 1, BLOCK), (nq + 1, 8, BLOCK)]
    whole = lambda s: pl.BlockSpec(s, lambda i, *_: (0, 0, 0))
    scratch = [
        pltpu.VMEM((GROUP * BLOCK, BLOCK), jnp.float32),
        pltpu.VMEM((GROUP * BLOCK, BLOCK), jnp.float32),
        pltpu.VMEM((GROUP * BLOCK, BLOCK), jnp.bfloat16),
        pltpu.VMEM((GROUP * BLOCK, BLOCK), jnp.bfloat16),
        pltpu.VMEM(q.shape, q.dtype),
        pltpu.VMEM((2 * own.shape[0],) + own.shape[1:], own.dtype),
    ]
    if last:
        scratch += [pltpu.VMEM(s, jnp.float32) for s in shapes]
        out_shape = jax.ShapeDtypeStruct(q.shape, jnp.bfloat16)
        out_specs = whole(q.shape)
    else:
        out_shape = [jax.ShapeDtypeStruct(s, jnp.float32) for s in shapes]
        out_specs = [whole(s) for s in shapes]
    scratch += [pltpu.SemaphoreType.DMA((6,))]
    args = [q, own, other] + ([] if first else list(state))
    return pl.pallas_call(
        functools.partial(attention_kernel, first, last),
        grid_spec=pltpu.PrefetchScalarGridSpec(
            num_scalar_prefetch=3,
            grid=(1,),
            in_specs=[hbm] * len(args),
            out_specs=out_specs,
            scratch_shapes=scratch,
        ),
        out_shape=out_shape,
        compiler_params=pltpu.CompilerParams(vmem_limit_bytes=VMEM),
        cost_estimate=pl.CostEstimate(
            flops=1_000_000, bytes_accessed=1, transcendentals=0
        ),
    )(chunks, lists, counts, *args)


def make_tables(match, place):
    nq, most = match.shape
    at = jnp.arange(most, dtype=jnp.int32)
    before = (at[:, None] < at[None, :])[None] & match[:, :, None]
    pos = jnp.sum(before.astype(jnp.int32), axis=1)
    hit = (pos[:, :, None] == at[None, None, :]) & match[:, :, None]
    lists = jnp.sum(jnp.where(hit, place[:, :, None], 0), axis=1)
    counts = jnp.sum(match.astype(jnp.int32), axis=1)
    steps = (counts + GROUP - 1) // GROUP
    row = jnp.arange(nq, dtype=jnp.int32)
    ends = jnp.sum(jnp.where(row[:, None] <= row[None, :], steps[:, None], 0), axis=0)
    t = jnp.arange(nq * ((most + GROUP - 1) // GROUP) + 6, dtype=jnp.int32)
    b = jnp.sum((t[:, None] >= ends[None, :]).astype(jnp.int32), axis=1)
    start = jnp.sum(jnp.where(row[None, :] < b[:, None], steps[None, :], 0), axis=1)
    c = jnp.where(b < nq, t - start, 0)
    chunks = jnp.concatenate([ends[-1:], b * 8 + c])
    lists = jnp.pad(lists, ((0, 1), (0, 0))).reshape(-1)
    return chunks, lists, jnp.pad(counts, (0, 1))


def local(queries, keys, values, key_blocks, key_count):
    seq_count, head_count = lax.axis_size("seq"), lax.axis_size("head")
    y = lax.axis_index("head")
    core = lax.axis_index("seq") % 2

    index = lambda place, c, yy: (place * 2 + c) * head_count + yy
    groups = [
        [index(place, c, yy) for yy in ys for place in range(PLACES)]
        for c in range(2)
        for ys in ((0, 3), (1, 2))
    ]
    swap = lambda a: lax.all_to_all(
        a, ("seq", "head"), 0, 0, axis_index_groups=groups, tiled=True
    )
    to_core = lambda a: lax.ppermute(a, "seq", [(i, i ^ 1) for i in range(seq_count)])
    to_pair = lambda a: lax.ppermute(a, "head", [(i, i ^ 1) for i in range(head_count)])

    odd = (y >= 2).astype(jnp.int32)
    mine = jnp.concatenate([key_blocks[0], key_count[0][:, None]], axis=1)
    mine = jnp.where(core == odd, mine, to_core(mine))
    outer = (y == 0) | (y == 3)
    mine = mine.reshape(head_count, PLACES, 2, -1)
    mine = lax.dynamic_index_in_dim(mine, core, 2, keepdims=False)
    mine = jnp.where(outer, mine[0::3], mine[1:3]).reshape(2 * PLACES, -1)
    blocks, count = mine[:, :-1], mine[:, -1]
    active = jnp.arange(blocks.shape[1], dtype=jnp.int32)[None, :] < count[:, None]
    block_y = blocks // 32
    block_core = (blocks % 2) ^ core
    block_place = (blocks // 2) % PLACES
    near = ((block_y == 0) | (block_y == 3)) == outer
    block_at = (block_core * 2 + block_y // 2) * PLACES + block_place
    near_tables = make_tables(active & near, block_at)
    far_tables = make_tables(active & ~near, block_at)

    kv = swap(pack_kv(keys, values).reshape(2 * PLACES, 2, BLOCK, HDIM))
    kv_far = to_pair(kv)
    q, near_tables, far_tables = lax.optimization_barrier(
        (pack_q(queries), near_tables, far_tables)
    )
    q = swap(q.reshape(2 * PLACES, BLOCK, HDIM))
    state = attention(near_tables, q, kv, to_core(kv), None, False)
    state, kv_far = lax.optimization_barrier((state, kv_far))
    out = attention(far_tables, q, kv_far, to_core(kv_far), state, True)
    return unpack(swap(out).reshape(2, PLACES, BLOCK, HDIM))


def solution(mesh):
    placed = (
        P(("head", "seq"), None),
        P(("head", "seq"), None),
        P(("head", "seq"), None),
        P("seq", None, None),
        P("seq", None),
    )
    return jax.shard_map(
        local, mesh=mesh, in_specs=placed, out_specs=P(("head", "seq"), None), check_vma=False
    )
```

```python
import functools

import jax
import jax.numpy as jnp
from jax import lax
from jax.experimental import pallas as pl
from jax.experimental.pallas import tpu as pltpu
from jax.sharding import PartitionSpec as P

BLOCK = 128
HDIM = 128
LOG2E = 1.4426950408889634
FACTOR = LOG2E / HDIM**0.5
GROUP = 8
PLACES = 16
VMEM = 24 << 20


def pack_kv_kernel(k_ref, v_ref, o_ref):
    for h in range(o_ref.shape[0] * o_ref.shape[1]):
        cols = slice(h * HDIM, (h + 1) * HDIM)
        o_ref[h % 2, h // 2, 0] = k_ref[:, cols]
        o_ref[h % 2, h // 2, 1] = v_ref[:, cols].T


def pack_q_kernel(q_ref, o_ref):
    for h in range(o_ref.shape[0] * o_ref.shape[1]):
        o_ref[h % 2, h // 2] = q_ref[:, h * HDIM : (h + 1) * HDIM]


def unpack_kernel(x_ref, o_ref):
    for h in range(x_ref.shape[0] * x_ref.shape[1]):
        o_ref[:, h * HDIM : (h + 1) * HDIM] = x_ref[h % 2, h // 2]


STEP = 8
FLAT = pl.BlockSpec((BLOCK, 2 * STEP * HDIM), lambda i: (0, i))
PACKED = pl.BlockSpec((2, STEP, BLOCK, HDIM), lambda i: (0, i, 0, 0))


def pack_kv(keys, values):
    return pl.pallas_call(
        pack_kv_kernel,
        grid=(PLACES // STEP,),
        in_specs=[FLAT, FLAT],
        out_specs=pl.BlockSpec((2, STEP, 2, BLOCK, HDIM), lambda i: (0, i, 0, 0, 0)),
        out_shape=jax.ShapeDtypeStruct((2, PLACES, 2, BLOCK, HDIM), keys.dtype),
    )(keys, values)


def pack_q(queries):
    return pl.pallas_call(
        pack_q_kernel,
        grid=(PLACES // STEP,),
        in_specs=[FLAT],
        out_specs=PACKED,
        out_shape=jax.ShapeDtypeStruct((2, PLACES, BLOCK, HDIM), queries.dtype),
    )(queries)


def unpack(x):
    return pl.pallas_call(
        unpack_kernel,
        grid=(PLACES // STEP,),
        in_specs=[PACKED],
        out_specs=FLAT,
        out_shape=jax.ShapeDtypeStruct((BLOCK, 2 * PLACES * HDIM), x.dtype),
    )(x)


def attention_kernel(
    first, last, chunks, lists, counts, q_hbm, own_hbm, other_hbm, *rest
):
    rest = list(rest)
    if not first:
        acc_in, top_in, total_in = (rest.pop(0) for _ in range(3))
    if last:
        o_ref = rest.pop(0)
        acc_ref, top_ref, total_ref = rest[6:9]
    else:
        acc_ref, top_ref, total_ref = (rest.pop(0) for _ in range(3))
    s0, s1, p0, p1, q_ref, kv_ref = rest[:6]
    sems = rest[-1]
    nq = q_hbm.shape[0]
    half = own_hbm.shape[0]
    most = lists.shape[0] // (nq + 1)

    copies = [
        (q_hbm, q_ref),
        (own_hbm, kv_ref.at[pl.ds(0, half)]),
        (other_hbm, kv_ref.at[pl.ds(half, half)]),
    ]
    if not first:
        copies += [(acc_in, acc_ref), (top_in, top_ref), (total_in, total_ref)]
    copies = [
        pltpu.make_async_copy(src, dst, sems.at[i]) for i, (src, dst) in enumerate(copies)
    ]
    for copy in copies:
        copy.start()
    if first:
        acc_ref[...] = jnp.zeros_like(acc_ref)
        top_ref[...] = jnp.full_like(top_ref, -jnp.inf)
        total_ref[...] = jnp.zeros_like(total_ref)
    for copy in copies:
        copy.wait()

    def where(t):
        code = chunks[t + 1]
        return code // 8, code % 8

    def places(b, c):
        end = jnp.maximum(counts[b] - 1, 0)
        return [lists[b * most + jnp.minimum(c * GROUP + g, end)] for g in range(GROUP)]

    def scores(b, chosen, dst):
        rows = jnp.concatenate([kv_ref[i, 0] for i in chosen], axis=0)
        q = q_ref[jnp.minimum(b, nq - 1)]
        s = lax.dot_general(rows, q, (((1,), (1,)), ((), ())), preferred_element_type=jnp.float32)
        dst[...] = s
        return jnp.max(s.reshape(GROUP * BLOCK // 8, 8, BLOCK), axis=0)

    def weights(b, c, largest, src, dst, top, total):
        count = counts[b]
        top = jnp.where(c == 0, top_ref[b], top)
        total = jnp.where(c == 0, total_ref[b], total)
        new_top = jnp.maximum(top, jnp.max(largest, axis=0, keepdims=True) * FACTOR)
        shrink = jnp.exp2(top - new_top)
        total = total * shrink
        for g in range(GROUP):
            rows = slice(g * BLOCK, (g + 1) * BLOCK)
            base = jnp.where(c * GROUP + g < count, new_top, jnp.inf)
            weight = jnp.exp2(src[rows, :] * FACTOR - base)
            total = total + jnp.sum(weight.reshape(BLOCK // 8, 8, BLOCK), axis=0)
            dst[rows, :] = weight.astype(jnp.bfloat16)
        top_ref[b] = new_top
        total_ref[b] = total
        return new_top, total, shrink

    def weighted(b, chosen, shrink, src):
        cols = jnp.concatenate([kv_ref[i, 1] for i in chosen], axis=1)
        acc_ref[b] = acc_ref[b] * shrink + jnp.dot(
            cols, src[...], preferred_element_type=jnp.float32
        )

    steps = chunks[0]
    score_bufs, weight_bufs = (s0, s1), (p0, p1)
    b0, c0 = where(0)
    places0 = places(b0, c0)
    largest0 = scores(b0, places0, s0)
    b1, c1 = where(1)
    places1 = places(b1, c1)
    largest1 = scores(b1, places1, s1)
    top, total, shrink0 = weights(
        b0,
        c0,
        largest0,
        s0,
        p0,
        jnp.full((1, BLOCK), -jnp.inf, jnp.float32),
        jnp.zeros((8, BLOCK), jnp.float32),
    )

    def body(i, carry):
        b0, shrink0, b1, c1, largest1, top, total = carry[:7]
        places0, places1 = list(carry[7 : 7 + GROUP]), list(carry[7 + GROUP :])
        for u in range(4):
            b2, c2 = where(4 * i + u + 2)
            places2 = places(b2, c2)
            largest2 = scores(b2, places2, score_bufs[u % 2])
            top, total, shrink1 = weights(
                b1, c1, largest1, score_bufs[1 - u % 2], weight_bufs[1 - u % 2], top, total
            )
            weighted(b0, places0, shrink0, weight_bufs[u % 2])
            b0, shrink0, places0 = b1, shrink1, places1
            b1, c1, largest1, places1 = b2, c2, largest2, places2
        return (b0, shrink0, b1, c1, largest1, top, total, *places0, *places1)

    lax.fori_loop(
        0,
        (steps + 3) // 4,
        body,
        (b0, shrink0, b1, c1, largest1, top, total, *places0, *places1),
    )

    if last:

        def finish(b, _):
            out = acc_ref[b] / jnp.sum(total_ref[b], axis=0, keepdims=True)
            o_ref[b] = out.T.astype(jnp.bfloat16)
            return 0

        lax.fori_loop(0, nq, finish, 0, unroll=4)


def attention(tables, q, own, other, state, last):
    chunks, lists, counts = tables
    nq = q.shape[0]
    first = state is None
    hbm = pl.BlockSpec(memory_space=pl.ANY)
    shapes = [(nq + 1, HDIM, BLOCK), (nq + 1, 1, BLOCK), (nq + 1, 8, BLOCK)]
    whole = lambda s: pl.BlockSpec(s, lambda i, *_: (0, 0, 0))
    scratch = [
        pltpu.VMEM((GROUP * BLOCK, BLOCK), jnp.float32),
        pltpu.VMEM((GROUP * BLOCK, BLOCK), jnp.float32),
        pltpu.VMEM((GROUP * BLOCK, BLOCK), jnp.bfloat16),
        pltpu.VMEM((GROUP * BLOCK, BLOCK), jnp.bfloat16),
        pltpu.VMEM(q.shape, q.dtype),
        pltpu.VMEM((2 * own.shape[0],) + own.shape[1:], own.dtype),
    ]
    if last:
        scratch += [pltpu.VMEM(s, jnp.float32) for s in shapes]
        out_shape = jax.ShapeDtypeStruct(q.shape, jnp.bfloat16)
        out_specs = whole(q.shape)
    else:
        out_shape = [jax.ShapeDtypeStruct(s, jnp.float32) for s in shapes]
        out_specs = [whole(s) for s in shapes]
    scratch += [pltpu.SemaphoreType.DMA((6,))]
    args = [q, own, other] + ([] if first else list(state))
    return pl.pallas_call(
        functools.partial(attention_kernel, first, last),
        grid_spec=pltpu.PrefetchScalarGridSpec(
            num_scalar_prefetch=3,
            grid=(1,),
            in_specs=[hbm] * len(args),
            out_specs=out_specs,
            scratch_shapes=scratch,
        ),
        out_shape=out_shape,
        compiler_params=pltpu.CompilerParams(vmem_limit_bytes=VMEM),
        cost_estimate=pl.CostEstimate(
            flops=1_000_000, bytes_accessed=1, transcendentals=0
        ),
    )(chunks, lists, counts, *args)


def make_tables(match, place):
    nq, most = match.shape
    at = jnp.arange(most, dtype=jnp.int32)
    before = (at[:, None] < at[None, :])[None] & match[:, :, None]
    pos = jnp.sum(before.astype(jnp.int32), axis=1)
    hit = (pos[:, :, None] == at[None, None, :]) & match[:, :, None]
    lists = jnp.sum(jnp.where(hit, place[:, :, None], 0), axis=1)
    counts = jnp.sum(match.astype(jnp.int32), axis=1)
    steps = (counts + GROUP - 1) // GROUP
    row = jnp.arange(nq, dtype=jnp.int32)
    ends = jnp.sum(jnp.where(row[:, None] <= row[None, :], steps[:, None], 0), axis=0)
    t = jnp.arange(nq * ((most + GROUP - 1) // GROUP) + 6, dtype=jnp.int32)
    b = jnp.sum((t[:, None] >= ends[None, :]).astype(jnp.int32), axis=1)
    start = jnp.sum(jnp.where(row[None, :] < b[:, None], steps[None, :], 0), axis=1)
    c = jnp.where(b < nq, t - start, 0)
    chunks = jnp.concatenate([ends[-1:], b * 8 + c])
    lists = jnp.pad(lists, ((0, 1), (0, 0))).reshape(-1)
    return chunks, lists, jnp.pad(counts, (0, 1))


def local(queries, keys, values, key_blocks, key_count):
    seq_count, head_count = lax.axis_size("seq"), lax.axis_size("head")
    y = lax.axis_index("head")
    core = lax.axis_index("seq") % 2

    index = lambda place, c, yy: (place * 2 + c) * head_count + yy
    groups = [
        [index(place, c, yy) for yy in ys for place in range(PLACES)]
        for c in range(2)
        for ys in ((0, 3), (1, 2))
    ]
    swap = lambda a: lax.all_to_all(
        a, ("seq", "head"), 0, 0, axis_index_groups=groups, tiled=True
    )
    to_core = lambda a: lax.ppermute(a, "seq", [(i, i ^ 1) for i in range(seq_count)])
    to_pair = lambda a: lax.ppermute(a, "head", [(i, i ^ 1) for i in range(head_count)])

    kv = pack_kv(keys, values)
    kv, key_blocks, key_count = lax.optimization_barrier((kv, key_blocks, key_count))

    odd = (y >= 2).astype(jnp.int32)
    mine = jnp.concatenate([key_blocks[0], key_count[0][:, None]], axis=1)
    mine = jnp.where(core == odd, mine, to_core(mine))
    outer = (y == 0) | (y == 3)
    mine = mine.reshape(head_count, PLACES, 2, -1)
    mine = lax.dynamic_index_in_dim(mine, core, 2, keepdims=False)
    mine = jnp.where(outer, mine[0::3], mine[1:3]).reshape(2 * PLACES, -1)
    blocks, count = mine[:, :-1], mine[:, -1]
    active = jnp.arange(blocks.shape[1], dtype=jnp.int32)[None, :] < count[:, None]
    block_y = blocks // 32
    block_core = (blocks % 2) ^ core
    block_place = (blocks // 2) % PLACES
    near = ((block_y == 0) | (block_y == 3)) == outer
    block_at = (block_core * 2 + block_y // 2) * PLACES + block_place
    near_tables = make_tables(active & near, block_at)
    far_tables = make_tables(active & ~near, block_at)

    kv, q, near_tables, far_tables = lax.optimization_barrier(
        (
            swap(kv.reshape(2 * PLACES, 2, BLOCK, HDIM)),
            pack_q(queries),
            near_tables,
            far_tables,
        )
    )
    kv_far = to_pair(kv)
    q = swap(q.reshape(2 * PLACES, BLOCK, HDIM))
    state = attention(near_tables, q, kv, to_core(kv), None, False)
    state, kv_far = lax.optimization_barrier((state, kv_far))
    out = attention(far_tables, q, kv_far, to_core(kv_far), state, True)
    return unpack(swap(out).reshape(2, PLACES, BLOCK, HDIM))


def solution(mesh):
    placed = (
        P(("head", "seq"), None),
        P(("head", "seq"), None),
        P(("head", "seq"), None),
        P("seq", None, None),
        P("seq", None),
    )
    return jax.shard_map(
        local, mesh=mesh, in_specs=placed, out_specs=P(("head", "seq"), None), check_vma=False
    )
```

```python
import functools

import jax
import jax.numpy as jnp
from jax import lax
from jax.experimental import pallas as pl
from jax.experimental.pallas import tpu as pltpu
from jax.sharding import PartitionSpec as P

BLOCK = 128
HDIM = 128
LOG2E = 1.4426950408889634
FACTOR = LOG2E / HDIM**0.5
CUT = 12
GROUP = 8
UNROLLS = (16, 4, 2)
PLACES = 16
VMEM = 24 << 20


def pack_kv_kernel(k_ref, v_ref, o_ref):
    for h in range(o_ref.shape[0] * o_ref.shape[1]):
        cols = slice(h * HDIM, (h + 1) * HDIM)
        o_ref[h % 2, h // 2, 0] = k_ref[:, cols]
        o_ref[h % 2, h // 2, 1] = v_ref[:, cols].T


def pack_q_kernel(q_ref, o_ref):
    for h in range(o_ref.shape[0] * o_ref.shape[1]):
        o_ref[h % 2, h // 2] = q_ref[:, h * HDIM : (h + 1) * HDIM]


def unpack_kernel(x_ref, o_ref):
    for h in range(x_ref.shape[0] * x_ref.shape[1]):
        o_ref[:, h * HDIM : (h + 1) * HDIM] = x_ref[h % 2, h // 2]


STEP = 8
FLAT = pl.BlockSpec((BLOCK, 2 * STEP * HDIM), lambda i: (0, i))
PACKED = pl.BlockSpec((2, STEP, BLOCK, HDIM), lambda i: (0, i, 0, 0))


def pack_kv(keys, values):
    return pl.pallas_call(
        pack_kv_kernel,
        grid=(PLACES // STEP,),
        in_specs=[FLAT, FLAT],
        out_specs=pl.BlockSpec((2, STEP, 2, BLOCK, HDIM), lambda i: (0, i, 0, 0, 0)),
        out_shape=jax.ShapeDtypeStruct((2, PLACES, 2, BLOCK, HDIM), keys.dtype),
    )(keys, values)


def pack_q(queries):
    return pl.pallas_call(
        pack_q_kernel,
        grid=(PLACES // STEP,),
        in_specs=[FLAT],
        out_specs=PACKED,
        out_shape=jax.ShapeDtypeStruct((2, PLACES, BLOCK, HDIM), queries.dtype),
    )(queries)


def unpack(x):
    return pl.pallas_call(
        unpack_kernel,
        grid=(PLACES // STEP,),
        in_specs=[PACKED],
        out_specs=FLAT,
        out_shape=jax.ShapeDtypeStruct((BLOCK, 2 * PLACES * HDIM), x.dtype),
    )(x)


def attention_kernel(
    first, last, parts, chunks, lists, counts, q_hbm, *rest
):
    rest = list(rest)
    kv_hbm = [rest.pop(0) for _ in range(parts)]
    if not first:
        acc_in, top_in, total_in = (rest.pop(0) for _ in range(3))
    if last:
        o_ref = rest.pop(0)
        acc_ref, top_ref, total_ref = rest[6:9]
    else:
        acc_ref, top_ref, total_ref = (rest.pop(0) for _ in range(3))
    s0, s1, p0, p1, q_ref, kv_ref = rest[:6]
    sems = rest[-1]
    nq = q_hbm.shape[0]
    most = lists.shape[0] // (nq + 1)

    copies = [(q_hbm, q_ref)]
    at = 0
    for part in kv_hbm:
        copies.append((part, kv_ref.at[pl.ds(at, part.shape[0])]))
        at += part.shape[0]
    if not first:
        copies += [(acc_in, acc_ref), (top_in, top_ref), (total_in, total_ref)]
    copies = [
        pltpu.make_async_copy(src, dst, sems.at[i]) for i, (src, dst) in enumerate(copies)
    ]
    for copy in copies:
        copy.start()
    if first:
        acc_ref[...] = jnp.zeros_like(acc_ref)
        top_ref[...] = jnp.full_like(top_ref, -jnp.inf)
        total_ref[...] = jnp.zeros_like(total_ref)
    for copy in copies:
        copy.wait()

    def where(t):
        code = chunks[t + 1]
        return code // 8, code % 8

    def places(b, c):
        end = jnp.maximum(counts[b] - 1, 0)
        return [lists[b * most + jnp.minimum(c * GROUP + g, end)] for g in range(GROUP)]

    def scores(b, chosen, dst):
        rows = jnp.concatenate([kv_ref[i, 0] for i in chosen], axis=0)
        q = q_ref[jnp.minimum(b, nq - 1)]
        s = lax.dot_general(rows, q, (((1,), (1,)), ((), ())), preferred_element_type=jnp.float32)
        dst[...] = s
        return jnp.max(s.reshape(GROUP * BLOCK // 8, 8, BLOCK), axis=0)

    def weights(b, c, largest, src, dst, top, total):
        count = counts[b]
        top = jnp.where(c == 0, top_ref[b], top)
        total = jnp.where(c == 0, total_ref[b], total)
        new_top = jnp.maximum(top, jnp.max(largest, axis=0, keepdims=True))
        shrink = jnp.exp2((top - new_top) * FACTOR)
        total = total * shrink
        for g in range(GROUP):
            rows = slice(g * BLOCK, (g + 1) * BLOCK)
            base = jnp.where(c * GROUP + g < count, new_top, jnp.inf)
            weight = jnp.exp2((src[rows, :] - base) * FACTOR)
            total = total + jnp.sum(weight.reshape(BLOCK // 8, 8, BLOCK), axis=0)
            dst[rows, :] = weight.astype(jnp.bfloat16)
        top_ref[b] = new_top
        total_ref[b] = total
        return new_top, total, shrink

    def weighted(b, chosen, shrink, src):
        cols = jnp.concatenate([kv_ref[i, 1] for i in chosen], axis=1)
        acc_ref[b] = acc_ref[b] * shrink + jnp.dot(
            cols, src[...], preferred_element_type=jnp.float32
        )

    steps = chunks[0]
    score_bufs, weight_bufs = (s0, s1), (p0, p1)
    b0, c0 = where(0)
    places0 = places(b0, c0)
    largest0 = scores(b0, places0, s0)
    b1, c1 = where(1)
    places1 = places(b1, c1)
    largest1 = scores(b1, places1, s1)
    top, total, shrink0 = weights(
        b0,
        c0,
        largest0,
        s0,
        p0,
        jnp.full((1, BLOCK), -jnp.inf, jnp.float32),
        jnp.zeros((8, BLOCK), jnp.float32),
    )

    def body(start, unroll):
        def run(i, carry):
            b0, shrink0, b1, c1, largest1, top, total = carry[:7]
            places0, places1 = list(carry[7 : 7 + GROUP]), list(carry[7 + GROUP :])
            for u in range(unroll):
                b2, c2 = where(start + unroll * i + u + 2)
                places2 = places(b2, c2)
                largest2 = scores(b2, places2, score_bufs[u % 2])
                top, total, shrink1 = weights(
                    b1, c1, largest1, score_bufs[1 - u % 2], weight_bufs[1 - u % 2], top, total
                )
                weighted(b0, places0, shrink0, weight_bufs[u % 2])
                b0, shrink0, places0 = b1, shrink1, places1
                b1, c1, largest1, places1 = b2, c2, largest2, places2
            return (b0, shrink0, b1, c1, largest1, top, total, *places0, *places1)

        return run

    state = (b0, shrink0, b1, c1, largest1, top, total, *places0, *places1)
    done = 0
    for unroll in UNROLLS:
        extra = 1 if unroll == UNROLLS[-1] else 0
        rounds = (steps - done + extra) // unroll
        state = lax.fori_loop(0, rounds, body(done, unroll), state)
        done = done + rounds * unroll

    if last:

        def finish(b, _):
            out = acc_ref[b] / jnp.sum(total_ref[b], axis=0, keepdims=True)
            o_ref[b] = out.T.astype(jnp.bfloat16)
            return 0

        lax.fori_loop(0, nq, finish, 0, unroll=4)


def attention(tables, q, kv, state, last):
    chunks, lists, counts = tables
    nq = q.shape[0]
    first = state is None
    hbm = pl.BlockSpec(memory_space=pl.ANY)
    shapes = [(nq + 1, HDIM, BLOCK), (nq + 1, 1, BLOCK), (nq + 1, 8, BLOCK)]
    whole = lambda s: pl.BlockSpec(s, lambda i, *_: (0, 0, 0))
    scratch = [
        pltpu.VMEM((GROUP * BLOCK, BLOCK), jnp.float32),
        pltpu.VMEM((GROUP * BLOCK, BLOCK), jnp.float32),
        pltpu.VMEM((GROUP * BLOCK, BLOCK), jnp.bfloat16),
        pltpu.VMEM((GROUP * BLOCK, BLOCK), jnp.bfloat16),
        pltpu.VMEM(q.shape, q.dtype),
        pltpu.VMEM((sum(a.shape[0] for a in kv),) + kv[0].shape[1:], kv[0].dtype),
    ]
    if last:
        scratch += [pltpu.VMEM(s, jnp.float32) for s in shapes]
        out_shape = jax.ShapeDtypeStruct(q.shape, jnp.bfloat16)
        out_specs = whole(q.shape)
    else:
        out_shape = [jax.ShapeDtypeStruct(s, jnp.float32) for s in shapes]
        out_specs = [whole(s) for s in shapes]
    scratch += [pltpu.SemaphoreType.DMA((8,))]
    args = [q, *kv] + ([] if first else list(state))
    return pl.pallas_call(
        functools.partial(attention_kernel, first, last, len(kv)),
        grid_spec=pltpu.PrefetchScalarGridSpec(
            num_scalar_prefetch=3,
            grid=(1,),
            in_specs=[hbm] * len(args),
            out_specs=out_specs,
            scratch_shapes=scratch,
        ),
        out_shape=out_shape,
        compiler_params=pltpu.CompilerParams(vmem_limit_bytes=VMEM),
        cost_estimate=pl.CostEstimate(
            flops=1_000_000, bytes_accessed=1, transcendentals=0
        ),
    )(chunks, lists, counts, *args)


def make_tables(match, place):
    nq, most = match.shape
    at = jnp.arange(most, dtype=jnp.int32)
    before = (at[:, None] < at[None, :])[None] & match[:, :, None]
    pos = jnp.sum(before.astype(jnp.int32), axis=1)
    hit = (pos[:, :, None] == at[None, None, :]) & match[:, :, None]
    lists = jnp.sum(jnp.where(hit, place[:, :, None], 0), axis=1)
    counts = jnp.sum(match.astype(jnp.int32), axis=1)
    steps = (counts + GROUP - 1) // GROUP
    row = jnp.arange(nq, dtype=jnp.int32)
    ends = jnp.sum(jnp.where(row[:, None] <= row[None, :], steps[:, None], 0), axis=0)
    t = jnp.arange(nq * ((most + GROUP - 1) // GROUP) + 4, dtype=jnp.int32)
    b = jnp.sum((t[:, None] >= ends[None, :]).astype(jnp.int32), axis=1)
    start = jnp.sum(jnp.where(row[None, :] < b[:, None], steps[None, :], 0), axis=1)
    c = jnp.where(b < nq, t - start, 0)
    chunks = jnp.concatenate([ends[-1:], b * 8 + c])
    lists = jnp.pad(lists, ((0, 1), (0, 0))).reshape(-1)
    return chunks, lists, jnp.pad(counts, (0, 1))


def local(queries, keys, values, key_blocks, key_count):
    seq_count, head_count = lax.axis_size("seq"), lax.axis_size("head")
    y = lax.axis_index("head")
    core = lax.axis_index("seq") % 2

    index = lambda place, c, yy: (place * 2 + c) * head_count + yy
    groups = [
        [index(place, c, yy) for yy in ys for place in range(PLACES)]
        for c in range(2)
        for ys in ((0, 3), (1, 2))
    ]
    swap = lambda a: lax.all_to_all(
        a, ("seq", "head"), 0, 0, axis_index_groups=groups, tiled=True
    )
    to_core = lambda a: lax.ppermute(a, "seq", [(i, i ^ 1) for i in range(seq_count)])
    to_pair = lambda a: lax.ppermute(a, "head", [(i, i ^ 1) for i in range(head_count)])

    kv = pack_kv(keys, values)
    kv, key_blocks, key_count = lax.optimization_barrier((kv, key_blocks, key_count))

    odd = (y >= 2).astype(jnp.int32)
    mine = jnp.concatenate([key_blocks[0], key_count[0][:, None]], axis=1)
    mine = jnp.where(core == odd, mine, to_core(mine))
    outer = (y == 0) | (y == 3)
    mine = mine.reshape(head_count, PLACES, 2, -1)
    mine = lax.dynamic_index_in_dim(mine, core, 2, keepdims=False)
    mine = jnp.where(outer, mine[0::3], mine[1:3]).reshape(2 * PLACES, -1)
    blocks, count = mine[:, :-1], mine[:, -1]
    active = jnp.arange(blocks.shape[1], dtype=jnp.int32)[None, :] < count[:, None]
    block_y = blocks // 32
    block_core = (blocks % 2) ^ core
    block_place = (blocks // 2) % PLACES
    near = ((block_y == 0) | (block_y == 3)) == outer
    block_at = (block_y // 2) * PLACES + block_place
    size = 2 * PLACES
    early = near | (block_at < CUT)
    early_place = jnp.where(
        near, block_core * size + block_at, 2 * size + block_core * CUT + block_at
    )
    late_place = block_core * (size - CUT) + block_at - CUT
    early_tables = make_tables(active & early, early_place)
    late_tables = make_tables(active & ~early, late_place)

    kv, q, early_tables, late_tables = lax.optimization_barrier(
        (
            swap(kv.reshape(2 * PLACES, 2, BLOCK, HDIM)),
            pack_q(queries),
            early_tables,
            late_tables,
        )
    )
    far, far_late = to_pair(kv[:CUT]), to_pair(kv[CUT:])
    q = swap(q.reshape(2 * PLACES, BLOCK, HDIM))
    state = attention(early_tables, q, [kv, to_core(kv), far, to_core(far)], None, False)
    state, far_late = lax.optimization_barrier((state, far_late))
    out = attention(late_tables, q, [far_late, to_core(far_late)], state, True)
    return unpack(swap(out).reshape(2, PLACES, BLOCK, HDIM))


def solution(mesh):
    placed = (
        P(("head", "seq"), None),
        P(("head", "seq"), None),
        P(("head", "seq"), None),
        P("seq", None, None),
        P("seq", None),
    )
    return jax.shard_map(
        local, mesh=mesh, in_specs=placed, out_specs=P(("head", "seq"), None), check_vma=False
    )
```

```python
import functools

import jax
import jax.numpy as jnp
from jax import lax
from jax.experimental import pallas as pl
from jax.experimental.pallas import tpu as pltpu
from jax.sharding import PartitionSpec as P

BLOCK = 128
HDIM = 128
LOG2E = 1.4426950408889634
FACTOR = LOG2E / HDIM**0.5
CUT = 14
GROUP = 4
UNROLLS = (32, 8, 2)
PLACES = 16
VMEM = 24 << 20


def pack_kv_kernel(k_ref, v_ref, o_ref):
    for h in range(o_ref.shape[0] * o_ref.shape[1]):
        cols = slice(h * HDIM, (h + 1) * HDIM)
        o_ref[h % 2, h // 2, 0] = k_ref[:, cols]
        o_ref[h % 2, h // 2, 1] = v_ref[:, cols].T


def pack_q_kernel(q_ref, o_ref):
    for h in range(o_ref.shape[0] * o_ref.shape[1]):
        o_ref[h % 2, h // 2] = q_ref[:, h * HDIM : (h + 1) * HDIM]


def unpack_kernel(x_ref, o_ref):
    for h in range(x_ref.shape[0] * x_ref.shape[1]):
        o_ref[:, h * HDIM : (h + 1) * HDIM] = x_ref[h % 2, h // 2]


STEP = 8
FLAT = pl.BlockSpec((BLOCK, 2 * STEP * HDIM), lambda i: (0, i))
PACKED = pl.BlockSpec((2, STEP, BLOCK, HDIM), lambda i: (0, i, 0, 0))


def pack_kv(keys, values):
    return pl.pallas_call(
        pack_kv_kernel,
        grid=(PLACES // STEP,),
        in_specs=[FLAT, FLAT],
        out_specs=pl.BlockSpec((2, STEP, 2, BLOCK, HDIM), lambda i: (0, i, 0, 0, 0)),
        out_shape=jax.ShapeDtypeStruct((2, PLACES, 2, BLOCK, HDIM), keys.dtype),
    )(keys, values)


def pack_q(queries):
    return pl.pallas_call(
        pack_q_kernel,
        grid=(PLACES // STEP,),
        in_specs=[FLAT],
        out_specs=PACKED,
        out_shape=jax.ShapeDtypeStruct((2, PLACES, BLOCK, HDIM), queries.dtype),
    )(queries)


def unpack(x):
    return pl.pallas_call(
        unpack_kernel,
        grid=(PLACES // STEP,),
        in_specs=[PACKED],
        out_specs=FLAT,
        out_shape=jax.ShapeDtypeStruct((BLOCK, 2 * PLACES * HDIM), x.dtype),
    )(x)


def attention_kernel(
    first, last, parts, chunks, lists, counts, q_ref, *rest
):
    rest = list(rest)
    kv_hbm = [rest.pop(0) for _ in range(parts)]
    if not first:
        acc_in, top_in, total_in = (rest.pop(0) for _ in range(3))
    if last:
        o_ref = rest.pop(0)
        acc_ref, top_ref, total_ref = rest[5:8]
    else:
        acc_ref, top_ref, total_ref = (rest.pop(0) for _ in range(3))
    s0, s1, p0, p1, kv_ref = rest[:5]
    sems = rest[-1]
    nq = q_ref.shape[0]
    most = lists.shape[0] // (nq + 1)

    copies = []
    at = 0
    for part in kv_hbm:
        copies.append((part, kv_ref.at[pl.ds(at, part.shape[0])]))
        at += part.shape[0]
    copies = [
        pltpu.make_async_copy(src, dst, sems.at[i]) for i, (src, dst) in enumerate(copies)
    ]
    for copy in copies:
        copy.start()
    if first:
        acc_ref[...] = jnp.zeros_like(acc_ref)
        top_ref[...] = jnp.full_like(top_ref, -jnp.inf)
        total_ref[...] = jnp.zeros_like(total_ref)
    else:
        acc_ref[...] = acc_in[...]
        top_ref[...] = top_in[...]
        total_ref[...] = total_in[...]
    for copy in copies:
        copy.wait()

    def where(t):
        code = chunks[t + 1]
        return code // 16, code % 16

    def places(b, c):
        end = jnp.maximum(counts[b] - 1, 0)
        return [lists[b * most + jnp.minimum(c * GROUP + g, end)] for g in range(GROUP)]

    def scores(b, chosen, dst):
        rows = jnp.concatenate([kv_ref[i, 0] for i in chosen], axis=0)
        q = q_ref[jnp.minimum(b, nq - 1)]
        s = lax.dot_general(rows, q, (((1,), (1,)), ((), ())), preferred_element_type=jnp.float32)
        dst[...] = s
        return jnp.max(s.reshape(GROUP * BLOCK // 8, 8, BLOCK), axis=0)

    def weights(b, c, largest, src, dst, top, total):
        count = counts[b]
        top = jnp.where(c == 0, top_ref[b], top)
        total = jnp.where(c == 0, total_ref[b], total)
        new_top = jnp.maximum(top, jnp.max(largest, axis=0, keepdims=True))
        shrink = jnp.exp2((top - new_top) * FACTOR)
        total = total * shrink
        for g in range(GROUP):
            rows = slice(g * BLOCK, (g + 1) * BLOCK)
            base = jnp.where(c * GROUP + g < count, new_top, jnp.inf)
            weight = jnp.exp2((src[rows, :] - base) * FACTOR)
            total = total + jnp.sum(weight.reshape(BLOCK // 8, 8, BLOCK), axis=0)
            dst[rows, :] = weight.astype(jnp.bfloat16)
        top_ref[b] = new_top
        total_ref[b] = total
        return new_top, total, shrink

    def weighted(b, chosen, shrink, src):
        cols = jnp.concatenate([kv_ref[i, 1] for i in chosen], axis=1)
        acc_ref[b] = acc_ref[b] * shrink + jnp.dot(
            cols, src[...], preferred_element_type=jnp.float32
        )

    steps = chunks[0]
    score_bufs, weight_bufs = (s0, s1), (p0, p1)
    b0, c0 = where(0)
    places0 = places(b0, c0)
    largest0 = scores(b0, places0, s0)
    b1, c1 = where(1)
    places1 = places(b1, c1)
    largest1 = scores(b1, places1, s1)
    top, total, shrink0 = weights(
        b0,
        c0,
        largest0,
        s0,
        p0,
        jnp.full((1, BLOCK), -jnp.inf, jnp.float32),
        jnp.zeros((8, BLOCK), jnp.float32),
    )

    def body(start, unroll):
        def run(i, carry):
            b0, shrink0, b1, c1, largest1, top, total = carry[:7]
            places0, places1 = list(carry[7 : 7 + GROUP]), list(carry[7 + GROUP :])
            for u in range(unroll):
                b2, c2 = where(start + unroll * i + u + 2)
                places2 = places(b2, c2)
                largest2 = scores(b2, places2, score_bufs[u % 2])
                top, total, shrink1 = weights(
                    b1, c1, largest1, score_bufs[1 - u % 2], weight_bufs[1 - u % 2], top, total
                )
                weighted(b0, places0, shrink0, weight_bufs[u % 2])
                b0, shrink0, places0 = b1, shrink1, places1
                b1, c1, largest1, places1 = b2, c2, largest2, places2
            return (b0, shrink0, b1, c1, largest1, top, total, *places0, *places1)

        return run

    state = (b0, shrink0, b1, c1, largest1, top, total, *places0, *places1)
    done = 0
    for unroll in UNROLLS:
        extra = 1 if unroll == UNROLLS[-1] else 0
        rounds = (steps - done + extra) // unroll
        state = lax.fori_loop(0, rounds, body(done, unroll), state)
        done = done + rounds * unroll

    if last:

        def finish(b, _):
            out = acc_ref[b] / jnp.sum(total_ref[b], axis=0, keepdims=True)
            o_ref[b] = out.T.astype(jnp.bfloat16)
            return 0

        lax.fori_loop(0, nq, finish, 0, unroll=4)


def attention(tables, q, kv, state, last):
    chunks, lists, counts = tables
    nq = q.shape[0]
    first = state is None
    hbm = pl.BlockSpec(memory_space=pl.ANY)
    shapes = [(nq + 1, HDIM, BLOCK), (nq + 1, 1, BLOCK), (nq + 1, 8, BLOCK)]
    vmem = pl.BlockSpec(memory_space=pltpu.VMEM)
    scratch = [
        pltpu.VMEM((GROUP * BLOCK, BLOCK), jnp.float32),
        pltpu.VMEM((GROUP * BLOCK, BLOCK), jnp.float32),
        pltpu.VMEM((GROUP * BLOCK, BLOCK), jnp.bfloat16),
        pltpu.VMEM((GROUP * BLOCK, BLOCK), jnp.bfloat16),
        pltpu.VMEM((sum(a.shape[0] for a in kv),) + kv[0].shape[1:], kv[0].dtype),
    ]
    if last:
        scratch += [pltpu.VMEM(s, jnp.float32) for s in shapes]
        out_shape = jax.ShapeDtypeStruct(q.shape, jnp.bfloat16)
        out_specs = vmem
    else:
        out_shape = [jax.ShapeDtypeStruct(s, jnp.float32) for s in shapes]
        out_specs = [vmem for s in shapes]
    scratch += [pltpu.SemaphoreType.DMA((len(kv),))]
    args = [q, *kv] + ([] if first else list(state))
    return pl.pallas_call(
        functools.partial(attention_kernel, first, last, len(kv)),
        grid_spec=pltpu.PrefetchScalarGridSpec(
            num_scalar_prefetch=3,
            grid=(1,),
            in_specs=[vmem] + [hbm] * len(kv) + [vmem] * (len(args) - 1 - len(kv)),
            out_specs=out_specs,
            scratch_shapes=scratch,
        ),
        out_shape=out_shape,
        compiler_params=pltpu.CompilerParams(vmem_limit_bytes=VMEM),
        cost_estimate=pl.CostEstimate(
            flops=1_000_000, bytes_accessed=1, transcendentals=0
        ),
    )(chunks, lists, counts, *args)


def make_tables(match, place):
    nq, most = match.shape
    at = jnp.arange(most, dtype=jnp.int32)
    before = (at[:, None] < at[None, :])[None] & match[:, :, None]
    pos = jnp.sum(before.astype(jnp.int32), axis=1)
    hit = (pos[:, :, None] == at[None, None, :]) & match[:, :, None]
    lists = jnp.sum(jnp.where(hit, place[:, :, None], 0), axis=1)
    counts = jnp.sum(match.astype(jnp.int32), axis=1)
    steps = (counts + GROUP - 1) // GROUP
    row = jnp.arange(nq, dtype=jnp.int32)
    ends = jnp.sum(jnp.where(row[:, None] <= row[None, :], steps[:, None], 0), axis=0)
    t = jnp.arange(nq * ((most + GROUP - 1) // GROUP) + 4, dtype=jnp.int32)
    b = jnp.sum((t[:, None] >= ends[None, :]).astype(jnp.int32), axis=1)
    start = jnp.sum(jnp.where(row[None, :] < b[:, None], steps[None, :], 0), axis=1)
    c = jnp.where(b < nq, t - start, 0)
    chunks = jnp.concatenate([ends[-1:], b * 16 + c])
    lists = jnp.pad(lists, ((0, 1), (0, 0))).reshape(-1)
    return chunks, lists, jnp.pad(counts, (0, 1))


def local(queries, keys, values, key_blocks, key_count):
    seq_count, head_count = lax.axis_size("seq"), lax.axis_size("head")
    y = lax.axis_index("head")
    core = lax.axis_index("seq") % 2

    index = lambda place, c, yy: (place * 2 + c) * head_count + yy
    groups = [
        [index(place, c, yy) for yy in ys for place in range(PLACES)]
        for c in range(2)
        for ys in ((0, 3), (1, 2))
    ]
    swap = lambda a: lax.all_to_all(
        a, ("seq", "head"), 0, 0, axis_index_groups=groups, tiled=True
    )
    to_core = lambda a: lax.ppermute(a, "seq", [(i, i ^ 1) for i in range(seq_count)])
    to_pair = lambda a: lax.ppermute(a, "head", [(i, i ^ 1) for i in range(head_count)])

    kv = pack_kv(keys, values)
    kv, key_blocks, key_count = lax.optimization_barrier((kv, key_blocks, key_count))

    odd = (y >= 2).astype(jnp.int32)
    mine = jnp.concatenate([key_blocks[0], key_count[0][:, None]], axis=1)
    mine = jnp.where(core == odd, mine, to_core(mine))
    outer = (y == 0) | (y == 3)
    mine = mine.reshape(head_count, PLACES, 2, -1)
    mine = lax.dynamic_index_in_dim(mine, core, 2, keepdims=False)
    mine = jnp.where(outer, mine[0::3], mine[1:3]).reshape(2 * PLACES, -1)
    blocks, count = mine[:, :-1], mine[:, -1]
    active = jnp.arange(blocks.shape[1], dtype=jnp.int32)[None, :] < count[:, None]
    block_y = blocks // 32
    block_core = (blocks % 2) ^ core
    block_place = (blocks // 2) % PLACES
    near = ((block_y == 0) | (block_y == 3)) == outer
    block_at = (block_y // 2) * PLACES + block_place
    size = 2 * PLACES
    early = near | (block_at < CUT)
    early_place = jnp.where(
        near, block_core * size + block_at, 2 * size + block_core * CUT + block_at
    )
    late_place = block_core * (size - CUT) + block_at - CUT
    early_tables = make_tables(active & early, early_place)
    late_tables = make_tables(active & ~early, late_place)

    kv, q, early_tables, late_tables = lax.optimization_barrier(
        (
            swap(kv.reshape(2 * PLACES, 2, BLOCK, HDIM)),
            pack_q(queries),
            early_tables,
            late_tables,
        )
    )
    far, far_late = kv[:CUT], kv[CUT:]
    kv, far_late = lax.optimization_barrier((kv, far_late))
    far, far_late = to_pair(far), to_pair(far_late)
    q = swap(q.reshape(2 * PLACES, BLOCK, HDIM))
    state = attention(early_tables, q, [kv, to_core(kv), far, to_core(far)], None, False)
    state, far_late = lax.optimization_barrier((state, far_late))
    out = attention(late_tables, q, [far_late, to_core(far_late)], state, True)
    return unpack(swap(out).reshape(2, PLACES, BLOCK, HDIM))


def solution(mesh):
    placed = (
        P(("head", "seq"), None),
        P(("head", "seq"), None),
        P(("head", "seq"), None),
        P("seq", None, None),
        P("seq", None),
    )
    return jax.shard_map(
        local, mesh=mesh, in_specs=placed, out_specs=P(("head", "seq"), None), check_vma=False
    )
```

```python
import functools

import jax
import jax.numpy as jnp
from jax import lax
from jax.experimental import pallas as pl
from jax.experimental.pallas import tpu as pltpu
from jax.sharding import PartitionSpec as P

BLOCK = 128
HDIM = 128
LOG2E = 1.4426950408889634
FACTOR = LOG2E / HDIM**0.5
CUT = 16
GROUP = 4
UNROLLS = (32, 8, 2)
PLACES = 16
VMEM = 24 << 20


def pack_kv_kernel(k_ref, v_ref, o_ref):
    for h in range(o_ref.shape[0] * o_ref.shape[1]):
        cols = slice(h * HDIM, (h + 1) * HDIM)
        o_ref[h % 2, h // 2, 0] = k_ref[:, cols]
        o_ref[h % 2, h // 2, 1] = v_ref[:, cols].T


def pack_q_kernel(q_ref, o_ref):
    for h in range(o_ref.shape[0] * o_ref.shape[1]):
        o_ref[h % 2, h // 2] = q_ref[:, h * HDIM : (h + 1) * HDIM]


def unpack_kernel(x_ref, o_ref):
    for h in range(x_ref.shape[0] * x_ref.shape[1]):
        o_ref[:, h * HDIM : (h + 1) * HDIM] = x_ref[h % 2, h // 2]


STEP = 8
FLAT = pl.BlockSpec((BLOCK, 2 * STEP * HDIM), lambda i: (0, i))
PACKED = pl.BlockSpec((2, STEP, BLOCK, HDIM), lambda i: (0, i, 0, 0))


def pack_kv(keys, values):
    return pl.pallas_call(
        pack_kv_kernel,
        grid=(PLACES // STEP,),
        in_specs=[FLAT, FLAT],
        out_specs=pl.BlockSpec((2, STEP, 2, BLOCK, HDIM), lambda i: (0, i, 0, 0, 0)),
        out_shape=jax.ShapeDtypeStruct((2, PLACES, 2, BLOCK, HDIM), keys.dtype),
    )(keys, values)


def pack_q(queries):
    return pl.pallas_call(
        pack_q_kernel,
        grid=(PLACES // STEP,),
        in_specs=[FLAT],
        out_specs=PACKED,
        out_shape=jax.ShapeDtypeStruct((2, PLACES, BLOCK, HDIM), queries.dtype),
    )(queries)


def unpack(x):
    return pl.pallas_call(
        unpack_kernel,
        grid=(PLACES // STEP,),
        in_specs=[PACKED],
        out_specs=FLAT,
        out_shape=jax.ShapeDtypeStruct((BLOCK, 2 * PLACES * HDIM), x.dtype),
    )(x)


def attention_kernel(
    first, last, parts, chunks, lists, counts, q_ref, *rest
):
    rest = list(rest)
    kv_hbm = [rest.pop(0) for _ in range(parts)]
    if not first:
        acc_in, top_in, total_in = (rest.pop(0) for _ in range(3))
    if last:
        o_ref = rest.pop(0)
        acc_ref, top_ref, total_ref = rest[5:8]
    else:
        acc_ref, top_ref, total_ref = (rest.pop(0) for _ in range(3))
    s0, s1, p0, p1, kv_ref = rest[:5]
    sems = rest[-1]
    nq = q_ref.shape[0]
    most = lists.shape[0] // (nq + 1)

    copies = []
    at = 0
    for part in kv_hbm:
        copies.append((part, kv_ref.at[pl.ds(at, part.shape[0])]))
        at += part.shape[0]
    copies = [
        pltpu.make_async_copy(src, dst, sems.at[i]) for i, (src, dst) in enumerate(copies)
    ]
    for copy in copies:
        copy.start()
    if first:
        acc_ref[...] = jnp.zeros_like(acc_ref)
        top_ref[...] = jnp.full_like(top_ref, -jnp.inf)
        total_ref[...] = jnp.zeros_like(total_ref)
    else:
        acc_ref[...] = acc_in[...]
        top_ref[...] = top_in[...]
        total_ref[...] = total_in[...]
    for copy in copies:
        copy.wait()

    def where(t):
        code = chunks[t + 1]
        return code // 16, code % 16

    def places(b, c):
        end = jnp.maximum(counts[b] - 1, 0)
        return [lists[b * most + jnp.minimum(c * GROUP + g, end)] for g in range(GROUP)]

    def scores(b, chosen, dst):
        rows = jnp.concatenate([kv_ref[i, 0] for i in chosen], axis=0)
        q = q_ref[jnp.minimum(b, nq - 1)]
        s = lax.dot_general(rows, q, (((1,), (1,)), ((), ())), preferred_element_type=jnp.float32)
        dst[...] = s
        return jnp.max(s.reshape(GROUP * BLOCK // 8, 8, BLOCK), axis=0)

    def weights(b, c, largest, src, dst, top, total):
        count = counts[b]
        top = jnp.where(c == 0, top_ref[b], top)
        total = jnp.where(c == 0, total_ref[b], total)
        new_top = jnp.maximum(top, jnp.max(largest, axis=0, keepdims=True))
        shrink = jnp.exp2((top - new_top) * FACTOR)
        total = total * shrink
        for g in range(GROUP):
            rows = slice(g * BLOCK, (g + 1) * BLOCK)
            base = jnp.where(c * GROUP + g < count, new_top, jnp.inf)
            weight = jnp.exp2((src[rows, :] - base) * FACTOR)
            total = total + jnp.sum(weight.reshape(BLOCK // 8, 8, BLOCK), axis=0)
            dst[rows, :] = weight.astype(jnp.bfloat16)
        top_ref[b] = new_top
        total_ref[b] = total
        return new_top, total, shrink

    def weighted(b, chosen, shrink, src):
        cols = jnp.concatenate([kv_ref[i, 1] for i in chosen], axis=1)
        acc_ref[b] = acc_ref[b] * shrink + jnp.dot(
            cols, src[...], preferred_element_type=jnp.float32
        )

    steps = chunks[0]
    score_bufs, weight_bufs = (s0, s1), (p0, p1)
    b0, c0 = where(0)
    places0 = places(b0, c0)
    largest0 = scores(b0, places0, s0)
    b1, c1 = where(1)
    places1 = places(b1, c1)
    largest1 = scores(b1, places1, s1)
    top, total, shrink0 = weights(
        b0,
        c0,
        largest0,
        s0,
        p0,
        jnp.full((1, BLOCK), -jnp.inf, jnp.float32),
        jnp.zeros((8, BLOCK), jnp.float32),
    )

    def body(start, unroll):
        def run(i, carry):
            b0, shrink0, b1, c1, largest1, top, total = carry[:7]
            places0, places1 = list(carry[7 : 7 + GROUP]), list(carry[7 + GROUP :])
            for u in range(unroll):
                b2, c2 = where(start + unroll * i + u + 2)
                places2 = places(b2, c2)
                largest2 = scores(b2, places2, score_bufs[u % 2])
                top, total, shrink1 = weights(
                    b1, c1, largest1, score_bufs[1 - u % 2], weight_bufs[1 - u % 2], top, total
                )
                weighted(b0, places0, shrink0, weight_bufs[u % 2])
                b0, shrink0, places0 = b1, shrink1, places1
                b1, c1, largest1, places1 = b2, c2, largest2, places2
            return (b0, shrink0, b1, c1, largest1, top, total, *places0, *places1)

        return run

    state = (b0, shrink0, b1, c1, largest1, top, total, *places0, *places1)
    done = 0
    for unroll in UNROLLS:
        extra = 1 if unroll == UNROLLS[-1] else 0
        rounds = (steps - done + extra) // unroll
        state = lax.fori_loop(0, rounds, body(done, unroll), state)
        done = done + rounds * unroll

    if last:

        def finish(b, _):
            out = acc_ref[b] / jnp.sum(total_ref[b], axis=0, keepdims=True)
            o_ref[b] = out.T.astype(jnp.bfloat16)
            return 0

        lax.fori_loop(0, nq, finish, 0, unroll=4)


def attention(tables, q, kv, state, last):
    chunks, lists, counts = tables
    nq = q.shape[0]
    first = state is None
    hbm = pl.BlockSpec(memory_space=pl.ANY)
    shapes = [(nq + 1, HDIM, BLOCK), (nq + 1, 1, BLOCK), (nq + 1, 8, BLOCK)]
    vmem = pl.BlockSpec(memory_space=pltpu.VMEM)
    scratch = [
        pltpu.VMEM((GROUP * BLOCK, BLOCK), jnp.float32),
        pltpu.VMEM((GROUP * BLOCK, BLOCK), jnp.float32),
        pltpu.VMEM((GROUP * BLOCK, BLOCK), jnp.bfloat16),
        pltpu.VMEM((GROUP * BLOCK, BLOCK), jnp.bfloat16),
        pltpu.VMEM((sum(a.shape[0] for a in kv),) + kv[0].shape[1:], kv[0].dtype),
    ]
    if last:
        scratch += [pltpu.VMEM(s, jnp.float32) for s in shapes]
        out_shape = jax.ShapeDtypeStruct(q.shape, jnp.bfloat16)
        out_specs = vmem
    else:
        out_shape = [jax.ShapeDtypeStruct(s, jnp.float32) for s in shapes]
        out_specs = [vmem for s in shapes]
    scratch += [pltpu.SemaphoreType.DMA((len(kv),))]
    args = [q, *kv] + ([] if first else list(state))
    return pl.pallas_call(
        functools.partial(attention_kernel, first, last, len(kv)),
        grid_spec=pltpu.PrefetchScalarGridSpec(
            num_scalar_prefetch=3,
            grid=(1,),
            in_specs=[vmem] + [hbm] * len(kv) + [vmem] * (len(args) - 1 - len(kv)),
            out_specs=out_specs,
            scratch_shapes=scratch,
        ),
        out_shape=out_shape,
        compiler_params=pltpu.CompilerParams(vmem_limit_bytes=VMEM),
        cost_estimate=pl.CostEstimate(
            flops=3_000_000_000, bytes_accessed=1, transcendentals=0
        ),
    )(chunks, lists, counts, *args)


def make_tables(match, place):
    nq, most = match.shape
    at = jnp.arange(most, dtype=jnp.int32)
    before = (at[:, None] < at[None, :])[None] & match[:, :, None]
    pos = jnp.sum(before.astype(jnp.int32), axis=1)
    hit = (pos[:, :, None] == at[None, None, :]) & match[:, :, None]
    lists = jnp.sum(jnp.where(hit, place[:, :, None], 0), axis=1)
    counts = jnp.sum(match.astype(jnp.int32), axis=1)
    steps = (counts + GROUP - 1) // GROUP
    row = jnp.arange(nq, dtype=jnp.int32)
    ends = jnp.sum(jnp.where(row[:, None] <= row[None, :], steps[:, None], 0), axis=0)
    t = jnp.arange(nq * ((most + GROUP - 1) // GROUP) + 4, dtype=jnp.int32)
    b = jnp.sum((t[:, None] >= ends[None, :]).astype(jnp.int32), axis=1)
    start = jnp.sum(jnp.where(row[None, :] < b[:, None], steps[None, :], 0), axis=1)
    c = jnp.where(b < nq, t - start, 0)
    chunks = jnp.concatenate([ends[-1:], b * 16 + c])
    lists = jnp.pad(lists, ((0, 1), (0, 0))).reshape(-1)
    return chunks, lists, jnp.pad(counts, (0, 1))


def local(queries, keys, values, key_blocks, key_count):
    seq_count, head_count = lax.axis_size("seq"), lax.axis_size("head")
    y = lax.axis_index("head")
    core = lax.axis_index("seq") % 2

    index = lambda place, c, yy: (place * 2 + c) * head_count + yy
    groups = [
        [index(place, c, yy) for yy in ys for place in range(PLACES)]
        for c in range(2)
        for ys in ((0, 3), (1, 2))
    ]
    swap = lambda a: lax.all_to_all(
        a, ("seq", "head"), 0, 0, axis_index_groups=groups, tiled=True
    )
    to_core = lambda a: lax.ppermute(a, "seq", [(i, i ^ 1) for i in range(seq_count)])
    to_pair = lambda a: lax.ppermute(a, "head", [(i, i ^ 1) for i in range(head_count)])

    kv = pack_kv(keys, values)
    kv, key_blocks, key_count = lax.optimization_barrier((kv, key_blocks, key_count))

    odd = (y >= 2).astype(jnp.int32)
    mine = jnp.concatenate([key_blocks[0], key_count[0][:, None]], axis=1)
    mine = jnp.where(core == odd, mine, to_core(mine))
    outer = (y == 0) | (y == 3)
    mine = mine.reshape(head_count, PLACES, 2, -1)
    mine = lax.dynamic_index_in_dim(mine, core, 2, keepdims=False)
    mine = jnp.where(outer, mine[0::3], mine[1:3]).reshape(2 * PLACES, -1)
    blocks, count = mine[:, :-1], mine[:, -1]
    active = jnp.arange(blocks.shape[1], dtype=jnp.int32)[None, :] < count[:, None]
    block_y = blocks // 32
    block_core = (blocks % 2) ^ core
    block_place = (blocks // 2) % PLACES
    near = ((block_y == 0) | (block_y == 3)) == outer
    block_at = (block_y // 2) * PLACES + block_place
    size = 2 * PLACES
    early = near | (block_at < CUT)
    early_place = jnp.where(
        near, block_core * size + block_at, 2 * size + block_core * CUT + block_at
    )
    late_place = block_core * (size - CUT) + block_at - CUT
    early_tables = make_tables(active & early, early_place)
    late_tables = make_tables(active & ~early, late_place)

    kv, q, early_tables, late_tables = lax.optimization_barrier(
        (
            swap(kv.reshape(2 * PLACES, 2, BLOCK, HDIM)),
            pack_q(queries),
            early_tables,
            late_tables,
        )
    )
    far, far_late = kv[:CUT], kv[CUT:]
    kv, far_late = lax.optimization_barrier((kv, far_late))
    far, far_late = to_pair(far), to_pair(far_late)
    q = swap(q.reshape(2 * PLACES, BLOCK, HDIM))
    state = attention(early_tables, q, [kv, to_core(kv), far, to_core(far)], None, False)
    state, far_late = lax.optimization_barrier((state, far_late))
    out = attention(late_tables, q, [far_late, to_core(far_late)], state, True)
    return unpack(swap(out).reshape(2, PLACES, BLOCK, HDIM))


def solution(mesh):
    placed = (
        P(("head", "seq"), None),
        P(("head", "seq"), None),
        P(("head", "seq"), None),
        P("seq", None, None),
        P("seq", None),
    )
    return jax.shard_map(
        local, mesh=mesh, in_specs=placed, out_specs=P(("head", "seq"), None), check_vma=False
    )
```

```python
import functools

import jax
import jax.numpy as jnp
from jax import lax
from jax.experimental import pallas as pl
from jax.experimental.pallas import tpu as pltpu
from jax.sharding import PartitionSpec as P

BLOCK = 128
HDIM = 128
LOG2E = 1.4426950408889634
FACTOR = LOG2E / HDIM**0.5
CUT = 15
GROUP = 4
UNROLLS = (32, 8, 2)
PLACES = 16
VMEM = 24 << 20


def pack_kv_kernel(k_ref, v_ref, o_ref):
    for h in range(o_ref.shape[0] * o_ref.shape[1]):
        cols = slice(h * HDIM, (h + 1) * HDIM)
        o_ref[h % 2, h // 2, 0] = k_ref[:, cols]
        o_ref[h % 2, h // 2, 1] = v_ref[:, cols].T


def pack_q_kernel(q_ref, o_ref):
    for h in range(o_ref.shape[0] * o_ref.shape[1]):
        o_ref[h % 2, h // 2] = q_ref[:, h * HDIM : (h + 1) * HDIM]


def unpack_kernel(x_ref, o_ref):
    for h in range(x_ref.shape[0] * x_ref.shape[1]):
        o_ref[:, h * HDIM : (h + 1) * HDIM] = x_ref[h % 2, h // 2]


STEP = 8
FLAT = pl.BlockSpec((BLOCK, 2 * STEP * HDIM), lambda i: (0, i))
PACKED = pl.BlockSpec((2, STEP, BLOCK, HDIM), lambda i: (0, i, 0, 0))


def pack_kv(keys, values):
    return pl.pallas_call(
        pack_kv_kernel,
        grid=(PLACES // STEP,),
        in_specs=[FLAT, FLAT],
        out_specs=pl.BlockSpec((2, STEP, 2, BLOCK, HDIM), lambda i: (0, i, 0, 0, 0)),
        out_shape=jax.ShapeDtypeStruct((2, PLACES, 2, BLOCK, HDIM), keys.dtype),
    )(keys, values)


def pack_q(queries):
    return pl.pallas_call(
        pack_q_kernel,
        grid=(PLACES // STEP,),
        in_specs=[FLAT],
        out_specs=PACKED,
        out_shape=jax.ShapeDtypeStruct((2, PLACES, BLOCK, HDIM), queries.dtype),
    )(queries)


def unpack(x):
    return pl.pallas_call(
        unpack_kernel,
        grid=(PLACES // STEP,),
        in_specs=[PACKED],
        out_specs=FLAT,
        out_shape=jax.ShapeDtypeStruct((BLOCK, 2 * PLACES * HDIM), x.dtype),
    )(x)


def attention_kernel(
    first, last, parts, chunks, lists, counts, q_ref, *rest
):
    rest = list(rest)
    kv_hbm = [rest.pop(0) for _ in range(parts)]
    if not first:
        acc_in, top_in, total_in = (rest.pop(0) for _ in range(3))
    if last:
        o_ref = rest.pop(0)
        acc_ref, top_ref, total_ref = rest[5:8]
    else:
        acc_ref, top_ref, total_ref = (rest.pop(0) for _ in range(3))
    s0, s1, p0, p1, kv_ref = rest[:5]
    sems = rest[-1]
    nq = q_ref.shape[0]
    most = lists.shape[0] // (nq + 1)

    copies = []
    at = 0
    for part in kv_hbm:
        copies.append((part, kv_ref.at[pl.ds(at, part.shape[0])]))
        at += part.shape[0]
    copies = [
        pltpu.make_async_copy(src, dst, sems.at[i]) for i, (src, dst) in enumerate(copies)
    ]
    for copy in copies:
        copy.start()
    if first:
        acc_ref[...] = jnp.zeros_like(acc_ref)
        top_ref[...] = jnp.full_like(top_ref, -jnp.inf)
        total_ref[...] = jnp.zeros_like(total_ref)
    else:
        acc_ref[...] = acc_in[...]
        top_ref[...] = top_in[...]
        total_ref[...] = total_in[...]
    for copy in copies:
        copy.wait()

    def where(t):
        code = chunks[t + 1]
        return code // 16, code % 16

    def places(b, c):
        end = jnp.maximum(counts[b] - 1, 0)
        return [lists[b * most + jnp.minimum(c * GROUP + g, end)] for g in range(GROUP)]

    def scores(b, chosen, dst):
        rows = jnp.concatenate([kv_ref[i, 0] for i in chosen], axis=0)
        q = q_ref[jnp.minimum(b, nq - 1)]
        s = lax.dot_general(rows, q, (((1,), (1,)), ((), ())), preferred_element_type=jnp.float32)
        dst[...] = s
        return jnp.max(s.reshape(GROUP * BLOCK // 8, 8, BLOCK), axis=0)

    def weights(b, c, largest, src, dst, top, total):
        count = counts[b]
        top = jnp.where(c == 0, top_ref[b], top)
        total = jnp.where(c == 0, total_ref[b], total)
        new_top = jnp.maximum(top, jnp.max(largest, axis=0, keepdims=True))
        shrink = jnp.exp2((top - new_top) * FACTOR)
        total = total * shrink
        for g in range(GROUP):
            rows = slice(g * BLOCK, (g + 1) * BLOCK)
            base = jnp.where(c * GROUP + g < count, new_top, jnp.inf)
            weight = jnp.exp2((src[rows, :] - base) * FACTOR)
            total = total + jnp.sum(weight.reshape(BLOCK // 8, 8, BLOCK), axis=0)
            dst[rows, :] = weight.astype(jnp.bfloat16)
        top_ref[b] = new_top
        total_ref[b] = total
        return new_top, total, shrink

    def weighted(b, chosen, shrink, src):
        cols = jnp.concatenate([kv_ref[i, 1] for i in chosen], axis=1)
        acc_ref[b] = acc_ref[b] * shrink + jnp.dot(
            cols, src[...], preferred_element_type=jnp.float32
        )

    steps = chunks[0]
    score_bufs, weight_bufs = (s0, s1), (p0, p1)
    b0, c0 = where(0)
    places0 = places(b0, c0)
    largest0 = scores(b0, places0, s0)
    b1, c1 = where(1)
    places1 = places(b1, c1)
    largest1 = scores(b1, places1, s1)
    top, total, shrink0 = weights(
        b0,
        c0,
        largest0,
        s0,
        p0,
        jnp.full((1, BLOCK), -jnp.inf, jnp.float32),
        jnp.zeros((8, BLOCK), jnp.float32),
    )

    def body(start, unroll):
        def run(i, carry):
            b0, shrink0, b1, c1, largest1, top, total = carry[:7]
            places0, places1 = list(carry[7 : 7 + GROUP]), list(carry[7 + GROUP :])
            for u in range(unroll):
                b2, c2 = where(start + unroll * i + u + 2)
                places2 = places(b2, c2)
                largest2 = scores(b2, places2, score_bufs[u % 2])
                top, total, shrink1 = weights(
                    b1, c1, largest1, score_bufs[1 - u % 2], weight_bufs[1 - u % 2], top, total
                )
                weighted(b0, places0, shrink0, weight_bufs[u % 2])
                b0, shrink0, places0 = b1, shrink1, places1
                b1, c1, largest1, places1 = b2, c2, largest2, places2
            return (b0, shrink0, b1, c1, largest1, top, total, *places0, *places1)

        return run

    state = (b0, shrink0, b1, c1, largest1, top, total, *places0, *places1)
    done = 0
    for unroll in UNROLLS:
        extra = 1 if unroll == UNROLLS[-1] else 0
        rounds = (steps - done + extra) // unroll
        state = lax.fori_loop(0, rounds, body(done, unroll), state)
        done = done + rounds * unroll

    if last:

        def finish(b, _):
            out = acc_ref[b] / jnp.sum(total_ref[b], axis=0, keepdims=True)
            o_ref[b] = out.T.astype(jnp.bfloat16)
            return 0

        lax.fori_loop(0, nq, finish, 0, unroll=4)


def attention(tables, q, kv, state, last):
    chunks, lists, counts = tables
    nq = q.shape[0]
    first = state is None
    hbm = pl.BlockSpec(memory_space=pl.ANY)
    shapes = [(nq + 1, HDIM, BLOCK), (nq + 1, 1, BLOCK), (nq + 1, 8, BLOCK)]
    vmem = pl.BlockSpec(memory_space=pltpu.VMEM)
    scratch = [
        pltpu.VMEM((GROUP * BLOCK, BLOCK), jnp.float32),
        pltpu.VMEM((GROUP * BLOCK, BLOCK), jnp.float32),
        pltpu.VMEM((GROUP * BLOCK, BLOCK), jnp.bfloat16),
        pltpu.VMEM((GROUP * BLOCK, BLOCK), jnp.bfloat16),
        pltpu.VMEM((sum(a.shape[0] for a in kv),) + kv[0].shape[1:], kv[0].dtype),
    ]
    if last:
        scratch += [pltpu.VMEM(s, jnp.float32) for s in shapes]
        out_shape = jax.ShapeDtypeStruct(q.shape, jnp.bfloat16)
        out_specs = vmem
    else:
        out_shape = [jax.ShapeDtypeStruct(s, jnp.float32) for s in shapes]
        out_specs = [vmem for s in shapes]
    scratch += [pltpu.SemaphoreType.DMA((len(kv),))]
    args = [q, *kv] + ([] if first else list(state))
    return pl.pallas_call(
        functools.partial(attention_kernel, first, last, len(kv)),
        grid_spec=pltpu.PrefetchScalarGridSpec(
            num_scalar_prefetch=3,
            grid=(1,),
            in_specs=[vmem] + [hbm] * len(kv) + [vmem] * (len(args) - 1 - len(kv)),
            out_specs=out_specs,
            scratch_shapes=scratch,
        ),
        out_shape=out_shape,
        compiler_params=pltpu.CompilerParams(vmem_limit_bytes=VMEM),
        cost_estimate=pl.CostEstimate(
            flops=5_000_000_000, bytes_accessed=1, transcendentals=0
        ),
    )(chunks, lists, counts, *args)


def make_tables(match, place):
    nq, most = match.shape
    at = jnp.arange(most, dtype=jnp.int32)
    before = (at[:, None] < at[None, :])[None] & match[:, :, None]
    pos = jnp.sum(before.astype(jnp.int32), axis=1)
    hit = (pos[:, :, None] == at[None, None, :]) & match[:, :, None]
    lists = jnp.sum(jnp.where(hit, place[:, :, None], 0), axis=1)
    counts = jnp.sum(match.astype(jnp.int32), axis=1)
    steps = (counts + GROUP - 1) // GROUP
    row = jnp.arange(nq, dtype=jnp.int32)
    ends = jnp.sum(jnp.where(row[:, None] <= row[None, :], steps[:, None], 0), axis=0)
    t = jnp.arange(nq * ((most + GROUP - 1) // GROUP) + 4, dtype=jnp.int32)
    b = jnp.sum((t[:, None] >= ends[None, :]).astype(jnp.int32), axis=1)
    start = jnp.sum(jnp.where(row[None, :] < b[:, None], steps[None, :], 0), axis=1)
    c = jnp.where(b < nq, t - start, 0)
    chunks = jnp.concatenate([ends[-1:], b * 16 + c])
    lists = jnp.pad(lists, ((0, 1), (0, 0))).reshape(-1)
    return chunks, lists, jnp.pad(counts, (0, 1))


def local(queries, keys, values, key_blocks, key_count):
    seq_count, head_count = lax.axis_size("seq"), lax.axis_size("head")
    y = lax.axis_index("head")
    core = lax.axis_index("seq") % 2

    index = lambda place, c, yy: (place * 2 + c) * head_count + yy
    groups = [
        [index(place, c, yy) for yy in ys for place in range(PLACES)]
        for c in range(2)
        for ys in ((0, 3), (1, 2))
    ]
    swap = lambda a: lax.all_to_all(
        a, ("seq", "head"), 0, 0, axis_index_groups=groups, tiled=True
    )
    to_core = lambda a: lax.ppermute(a, "seq", [(i, i ^ 1) for i in range(seq_count)])
    to_pair = lambda a: lax.ppermute(a, "head", [(i, i ^ 1) for i in range(head_count)])

    kv = pack_kv(keys, values)
    kv, key_blocks, key_count = lax.optimization_barrier((kv, key_blocks, key_count))

    odd = (y >= 2).astype(jnp.int32)
    mine = jnp.concatenate([key_blocks[0], key_count[0][:, None]], axis=1)
    mine = jnp.where(core == odd, mine, to_core(mine))
    outer = (y == 0) | (y == 3)
    mine = mine.reshape(head_count, PLACES, 2, -1)
    mine = lax.dynamic_index_in_dim(mine, core, 2, keepdims=False)
    mine = jnp.where(outer, mine[0::3], mine[1:3]).reshape(2 * PLACES, -1)
    blocks, count = mine[:, :-1], mine[:, -1]
    active = jnp.arange(blocks.shape[1], dtype=jnp.int32)[None, :] < count[:, None]
    block_y = blocks // 32
    block_core = (blocks % 2) ^ core
    block_place = (blocks // 2) % PLACES
    near = ((block_y == 0) | (block_y == 3)) == outer
    block_at = (block_y // 2) * PLACES + block_place
    size = 2 * PLACES
    early = near | (block_at < CUT)
    early_place = jnp.where(
        near, block_core * size + block_at, 2 * size + block_core * CUT + block_at
    )
    late_place = block_core * (size - CUT) + block_at - CUT
    early_tables = make_tables(active & early, early_place)
    late_tables = make_tables(active & ~early, late_place)

    kv, q, early_tables, late_tables = lax.optimization_barrier(
        (
            swap(kv.reshape(2 * PLACES, 2, BLOCK, HDIM)),
            pack_q(queries),
            early_tables,
            late_tables,
        )
    )
    far, far_late = kv[:CUT], kv[CUT:]
    kv, far_late = lax.optimization_barrier((kv, far_late))
    far, far_late = to_pair(far), to_pair(far_late)
    q = swap(q.reshape(2 * PLACES, BLOCK, HDIM))
    state = attention(early_tables, q, [kv, to_core(kv), far, to_core(far)], None, False)
    state, far_late = lax.optimization_barrier((state, far_late))
    out = attention(late_tables, q, [far_late, to_core(far_late)], state, True)
    return unpack(swap(out).reshape(2, PLACES, BLOCK, HDIM))


def solution(mesh):
    placed = (
        P(("head", "seq"), None),
        P(("head", "seq"), None),
        P(("head", "seq"), None),
        P("seq", None, None),
        P("seq", None),
    )
    return jax.shard_map(
        local, mesh=mesh, in_specs=placed, out_specs=P(("head", "seq"), None), check_vma=False
    )
```

```python
import functools

import jax
import jax.numpy as jnp
from jax import lax
from jax.experimental import pallas as pl
from jax.experimental.pallas import tpu as pltpu
from jax.sharding import PartitionSpec as P

BLOCK = 128
HDIM = 128
LOG2E = 1.4426950408889634
FACTOR = LOG2E / HDIM**0.5
CUT = 14
GROUP = 4
UNROLLS = (32, 8, 2)
PLACES = 16
VMEM = 24 << 20


def pack_kv_kernel(k_ref, v_ref, o_ref):
    for h in range(o_ref.shape[0] * o_ref.shape[1]):
        cols = slice(h * HDIM, (h + 1) * HDIM)
        o_ref[h % 2, h // 2, 0] = k_ref[:, cols]
        o_ref[h % 2, h // 2, 1] = v_ref[:, cols].T


def pack_q_kernel(q_ref, o_ref):
    for h in range(o_ref.shape[0] * o_ref.shape[1]):
        o_ref[h % 2, h // 2] = q_ref[:, h * HDIM : (h + 1) * HDIM]


def unpack_kernel(x_ref, o_ref):
    for h in range(x_ref.shape[0] * x_ref.shape[1]):
        o_ref[:, h * HDIM : (h + 1) * HDIM] = x_ref[h % 2, h // 2]


STEP = 8
FLAT = pl.BlockSpec((BLOCK, 2 * STEP * HDIM), lambda i: (0, i))
PACKED = pl.BlockSpec((2, STEP, BLOCK, HDIM), lambda i: (0, i, 0, 0))


def pack_kv(keys, values):
    return pl.pallas_call(
        pack_kv_kernel,
        grid=(PLACES // STEP,),
        in_specs=[FLAT, FLAT],
        out_specs=pl.BlockSpec((2, STEP, 2, BLOCK, HDIM), lambda i: (0, i, 0, 0, 0)),
        out_shape=jax.ShapeDtypeStruct((2, PLACES, 2, BLOCK, HDIM), keys.dtype),
    )(keys, values)


def pack_q(queries):
    return pl.pallas_call(
        pack_q_kernel,
        grid=(PLACES // STEP,),
        in_specs=[FLAT],
        out_specs=PACKED,
        out_shape=jax.ShapeDtypeStruct((2, PLACES, BLOCK, HDIM), queries.dtype),
    )(queries)


def unpack(x):
    return pl.pallas_call(
        unpack_kernel,
        grid=(PLACES // STEP,),
        in_specs=[PACKED],
        out_specs=FLAT,
        out_shape=jax.ShapeDtypeStruct((BLOCK, 2 * PLACES * HDIM), x.dtype),
    )(x)


def attention_kernel(
    first, last, parts, most, table_hbm, q_ref, *rest
):
    rest = list(rest)
    kv_hbm = [rest.pop(0) for _ in range(parts)]
    if not first:
        acc_in, top_in, total_in = (rest.pop(0) for _ in range(3))
    if last:
        o_ref = rest.pop(0)
        acc_ref, top_ref, total_ref = rest[5:8]
    else:
        acc_ref, top_ref, total_ref = (rest.pop(0) for _ in range(3))
    s0, s1, p0, p1, kv_ref = rest[:5]
    table, sems = rest[-2:]
    nq = q_ref.shape[0]

    copies = [(table_hbm, table)]
    at = 0
    for part in kv_hbm:
        copies.append((part, kv_ref.at[pl.ds(at, part.shape[0])]))
        at += part.shape[0]
    copies = [
        pltpu.make_async_copy(src, dst, sems.at[i]) for i, (src, dst) in enumerate(copies)
    ]
    for copy in copies:
        copy.start()
    if first:
        acc_ref[...] = jnp.zeros_like(acc_ref)
        top_ref[...] = jnp.full_like(top_ref, -jnp.inf)
        total_ref[...] = jnp.zeros_like(total_ref)
    else:
        acc_ref[...] = acc_in[...]
        top_ref[...] = top_in[...]
        total_ref[...] = total_in[...]
    for copy in copies:
        copy.wait()

    def where(t):
        code = table[t + (nq + 1) * (most + 1) + 1]
        return code // 16, code % 16

    def places(b, c):
        end = jnp.maximum(table[b] - 1, 0)
        return [table[(nq + 1) + b * most + jnp.minimum(c * GROUP + g, end)] for g in range(GROUP)]

    def scores(b, chosen, dst):
        rows = jnp.concatenate([kv_ref[i, 0] for i in chosen], axis=0)
        q = q_ref[jnp.minimum(b, nq - 1)]
        s = lax.dot_general(rows, q, (((1,), (1,)), ((), ())), preferred_element_type=jnp.float32)
        dst[...] = s
        return jnp.max(s.reshape(GROUP * BLOCK // 8, 8, BLOCK), axis=0)

    def weights(b, c, largest, src, dst, top, total):
        count = table[b]
        top = jnp.where(c == 0, top_ref[b], top)
        total = jnp.where(c == 0, total_ref[b], total)
        new_top = jnp.maximum(top, jnp.max(largest, axis=0, keepdims=True))
        shrink = jnp.exp2((top - new_top) * FACTOR)
        total = total * shrink
        for g in range(GROUP):
            rows = slice(g * BLOCK, (g + 1) * BLOCK)
            base = jnp.where(c * GROUP + g < count, new_top, jnp.inf)
            weight = jnp.exp2((src[rows, :] - base) * FACTOR)
            total = total + jnp.sum(weight.reshape(BLOCK // 8, 8, BLOCK), axis=0)
            dst[rows, :] = weight.astype(jnp.bfloat16)
        top_ref[b] = new_top
        total_ref[b] = total
        return new_top, total, shrink

    def weighted(b, chosen, shrink, src):
        cols = jnp.concatenate([kv_ref[i, 1] for i in chosen], axis=1)
        acc_ref[b] = acc_ref[b] * shrink + jnp.dot(
            cols, src[...], preferred_element_type=jnp.float32
        )

    steps = table[(nq + 1) * (most + 1)]
    score_bufs, weight_bufs = (s0, s1), (p0, p1)
    b0, c0 = where(0)
    places0 = places(b0, c0)
    largest0 = scores(b0, places0, s0)
    b1, c1 = where(1)
    places1 = places(b1, c1)
    largest1 = scores(b1, places1, s1)
    top, total, shrink0 = weights(
        b0,
        c0,
        largest0,
        s0,
        p0,
        jnp.full((1, BLOCK), -jnp.inf, jnp.float32),
        jnp.zeros((8, BLOCK), jnp.float32),
    )

    def body(start, unroll):
        def run(i, carry):
            b0, shrink0, b1, c1, largest1, top, total = carry[:7]
            places0, places1 = list(carry[7 : 7 + GROUP]), list(carry[7 + GROUP :])
            for u in range(unroll):
                b2, c2 = where(start + unroll * i + u + 2)
                places2 = places(b2, c2)
                largest2 = scores(b2, places2, score_bufs[u % 2])
                top, total, shrink1 = weights(
                    b1, c1, largest1, score_bufs[1 - u % 2], weight_bufs[1 - u % 2], top, total
                )
                weighted(b0, places0, shrink0, weight_bufs[u % 2])
                b0, shrink0, places0 = b1, shrink1, places1
                b1, c1, largest1, places1 = b2, c2, largest2, places2
            return (b0, shrink0, b1, c1, largest1, top, total, *places0, *places1)

        return run

    state = (b0, shrink0, b1, c1, largest1, top, total, *places0, *places1)
    done = 0
    for unroll in UNROLLS:
        extra = 1 if unroll == UNROLLS[-1] else 0
        rounds = (steps - done + extra) // unroll
        state = lax.fori_loop(0, rounds, body(done, unroll), state)
        done = done + rounds * unroll

    if last:

        def finish(b, _):
            out = acc_ref[b] * (1.0 / jnp.sum(total_ref[b], axis=0, keepdims=True))
            o_ref[b] = out.T.astype(jnp.bfloat16)
            return 0

        lax.fori_loop(0, nq, finish, 0, unroll=8)


def attention(table, most, q, kv, state, last):
    nq = q.shape[0]
    first = state is None
    hbm = pl.BlockSpec(memory_space=pl.ANY)
    shapes = [(nq + 1, HDIM, BLOCK), (nq + 1, 1, BLOCK), (nq + 1, 8, BLOCK)]
    vmem = pl.BlockSpec(memory_space=pltpu.VMEM)
    scratch = [
        pltpu.VMEM((GROUP * BLOCK, BLOCK), jnp.float32),
        pltpu.VMEM((GROUP * BLOCK, BLOCK), jnp.float32),
        pltpu.VMEM((GROUP * BLOCK, BLOCK), jnp.bfloat16),
        pltpu.VMEM((GROUP * BLOCK, BLOCK), jnp.bfloat16),
        pltpu.VMEM((sum(a.shape[0] for a in kv),) + kv[0].shape[1:], kv[0].dtype),
    ]
    if last:
        scratch += [pltpu.VMEM(s, jnp.float32) for s in shapes]
        out_shape = jax.ShapeDtypeStruct(q.shape, jnp.bfloat16)
        out_specs = vmem
    else:
        out_shape = [jax.ShapeDtypeStruct(s, jnp.float32) for s in shapes]
        out_specs = [vmem for s in shapes]
    scratch += [pltpu.SMEM(table.shape, jnp.int32), pltpu.SemaphoreType.DMA((len(kv) + 1,))]
    args = [q, *kv] + ([] if first else list(state))
    return pl.pallas_call(
        functools.partial(attention_kernel, first, last, len(kv), most),
        in_specs=[hbm, vmem] + [hbm] * len(kv) + [vmem] * (len(args) - 1 - len(kv)),
        out_specs=out_specs,
        scratch_shapes=scratch,
        out_shape=out_shape,
        compiler_params=pltpu.CompilerParams(vmem_limit_bytes=VMEM),
        cost_estimate=pl.CostEstimate(flops=1_000_000, bytes_accessed=1, transcendentals=0),
    )(table, *args)


def make_table(match, place):
    nq, most = match.shape
    at = jnp.arange(most, dtype=jnp.int32)
    before = (at[:, None] < at[None, :])[None] & match[:, :, None]
    pos = jnp.sum(before.astype(jnp.int32), axis=1)
    hit = (pos[:, :, None] == at[None, None, :]) & match[:, :, None]
    lists = jnp.sum(jnp.where(hit, place[:, :, None], 0), axis=1)
    counts = jnp.sum(match.astype(jnp.int32), axis=1)
    steps = (counts + GROUP - 1) // GROUP
    row = jnp.arange(nq, dtype=jnp.int32)
    ends = jnp.sum(jnp.where(row[:, None] <= row[None, :], steps[:, None], 0), axis=0)
    t = jnp.arange(nq * ((most + GROUP - 1) // GROUP) + 4, dtype=jnp.int32)
    b = jnp.sum((t[:, None] >= ends[None, :]).astype(jnp.int32), axis=1)
    start = jnp.sum(jnp.where(row[None, :] < b[:, None], steps[None, :], 0), axis=1)
    c = jnp.where(b < nq, t - start, 0)
    lists = jnp.pad(lists, ((0, 1), (0, 0))).reshape(-1)
    table = jnp.concatenate([jnp.pad(counts, (0, 1)), lists, ends[-1:], b * 16 + c])
    return jnp.pad(table, (0, -table.shape[0] % 1024))


def local(queries, keys, values, key_blocks, key_count):
    seq_count, head_count = lax.axis_size("seq"), lax.axis_size("head")
    y = lax.axis_index("head")
    core = lax.axis_index("seq") % 2

    index = lambda place, c, yy: (place * 2 + c) * head_count + yy
    groups = [
        [index(place, c, yy) for yy in ys for place in range(PLACES)]
        for c in range(2)
        for ys in ((0, 3), (1, 2))
    ]
    swap = lambda a: lax.all_to_all(
        a, ("seq", "head"), 0, 0, axis_index_groups=groups, tiled=True
    )
    to_core = lambda a: lax.ppermute(a, "seq", [(i, i ^ 1) for i in range(seq_count)])
    to_pair = lambda a: lax.ppermute(a, "head", [(i, i ^ 1) for i in range(head_count)])

    kv = pack_kv(keys, values)
    kv, key_blocks, key_count = lax.optimization_barrier((kv, key_blocks, key_count))

    odd = (y >= 2).astype(jnp.int32)
    mine = jnp.concatenate([key_blocks[0], key_count[0][:, None]], axis=1)
    mine = jnp.where(core == odd, mine, to_core(mine))
    outer = (y == 0) | (y == 3)
    mine = mine.reshape(head_count, PLACES, 2, -1)
    mine = lax.dynamic_index_in_dim(mine, core, 2, keepdims=False)
    mine = jnp.where(outer, mine[0::3], mine[1:3]).reshape(2 * PLACES, -1)
    blocks, count = mine[:, :-1], mine[:, -1]
    active = jnp.arange(blocks.shape[1], dtype=jnp.int32)[None, :] < count[:, None]
    block_y = blocks // 32
    block_core = (blocks % 2) ^ core
    block_place = (blocks // 2) % PLACES
    near = ((block_y == 0) | (block_y == 3)) == outer
    block_at = (block_y // 2) * PLACES + block_place
    size, most = 2 * PLACES, blocks.shape[1]
    early = near | (block_at < CUT)
    early_place = jnp.where(
        near, block_core * size + block_at, 2 * size + block_core * CUT + block_at
    )
    late_place = block_core * (size - CUT) + block_at - CUT
    early_table = make_table(active & early, early_place)
    late_table = make_table(active & ~early, late_place)

    kv, q, early_table, late_table = lax.optimization_barrier(
        (
            swap(kv.reshape(2 * PLACES, 2, BLOCK, HDIM)),
            pack_q(queries),
            early_table,
            late_table,
        )
    )
    far, far_late = kv[:CUT], kv[CUT:]
    kv, far_late = lax.optimization_barrier((kv, far_late))
    far, far_late = to_pair(far), to_pair(far_late)
    q = swap(q.reshape(2 * PLACES, BLOCK, HDIM))
    state = attention(early_table, most, q, [kv, to_core(kv), far, to_core(far)], None, False)
    state, far_late = lax.optimization_barrier((state, far_late))
    out = attention(late_table, most, q, [far_late, to_core(far_late)], state, True)
    return unpack(swap(out).reshape(2, PLACES, BLOCK, HDIM))


def solution(mesh):
    placed = (
        P(("head", "seq"), None),
        P(("head", "seq"), None),
        P(("head", "seq"), None),
        P("seq", None, None),
        P("seq", None),
    )
    return jax.shard_map(
        local, mesh=mesh, in_specs=placed, out_specs=P(("head", "seq"), None), check_vma=False
    )
```

```python
import functools

import jax
import jax.numpy as jnp
from jax import lax
from jax.experimental import pallas as pl
from jax.experimental.pallas import tpu as pltpu
from jax.sharding import PartitionSpec as P

BLOCK = 128
HDIM = 128
LOG2E = 1.4426950408889634
FACTOR = LOG2E / HDIM**0.5
CUT = 14
GROUP = 4
UNROLLS = (32, 8, 2)
PLACES = 16
VMEM = 24 << 20


def pack_kv_kernel(k_hbm, v_hbm, o_hbm, k_ref, v_ref, o_ref, in_sems, out_sems):
    parts = in_sems.shape[0]
    heads = 2 * PLACES // parts
    width = heads * HDIM
    places = heads // 2
    arrivals, departures = [], []
    for i in range(parts):
        cols = pl.ds(i * width, width)
        for j, (src, dst) in enumerate(((k_hbm, k_ref), (v_hbm, v_ref))):
            copy = pltpu.make_async_copy(src.at[:, cols], dst.at[:, cols], in_sems.at[i, j])
            copy.start()
            arrivals.append(copy)
    for i in range(parts):
        arrivals[2 * i].wait()
        arrivals[2 * i + 1].wait()
        for h in range(i * heads, (i + 1) * heads):
            cols = slice(h * HDIM, (h + 1) * HDIM)
            o_ref[h % 2, h // 2, 0] = k_ref[:, cols]
            o_ref[h % 2, h // 2, 1] = v_ref[:, cols].T
        at = pl.ds(i * places, places)
        copy = pltpu.make_async_copy(o_ref.at[:, at], o_hbm.at[:, at], out_sems.at[i])
        copy.start()
        departures.append(copy)
    for copy in departures:
        copy.wait()


def pack_q_kernel(q_ref, o_ref):
    for h in range(o_ref.shape[0] * o_ref.shape[1]):
        o_ref[h % 2, h // 2] = q_ref[:, h * HDIM : (h + 1) * HDIM]


def unpack_kernel(x_ref, o_ref):
    for h in range(x_ref.shape[0] * x_ref.shape[1]):
        o_ref[:, h * HDIM : (h + 1) * HDIM] = x_ref[h % 2, h // 2]


STEP = 8
FLAT = pl.BlockSpec((BLOCK, 2 * STEP * HDIM), lambda i: (0, i))
PACKED = pl.BlockSpec((2, STEP, BLOCK, HDIM), lambda i: (0, i, 0, 0))


def pack_kv(keys, values):
    hbm = pl.BlockSpec(memory_space=pl.ANY)
    shape = (2, PLACES, 2, BLOCK, HDIM)
    return pl.pallas_call(
        pack_kv_kernel,
        in_specs=[hbm, hbm],
        out_specs=hbm,
        out_shape=jax.ShapeDtypeStruct(shape, keys.dtype),
        scratch_shapes=[
            pltpu.VMEM(keys.shape, keys.dtype),
            pltpu.VMEM(values.shape, values.dtype),
            pltpu.VMEM(shape, keys.dtype),
            pltpu.SemaphoreType.DMA((4, 2)),
            pltpu.SemaphoreType.DMA((4,)),
        ],
        compiler_params=pltpu.CompilerParams(vmem_limit_bytes=VMEM),
    )(keys, values)


def pack_q(queries):
    return pl.pallas_call(
        pack_q_kernel,
        grid=(PLACES // STEP,),
        in_specs=[FLAT],
        out_specs=PACKED,
        out_shape=jax.ShapeDtypeStruct((2, PLACES, BLOCK, HDIM), queries.dtype),
    )(queries)


def unpack(x):
    return pl.pallas_call(
        unpack_kernel,
        grid=(PLACES // STEP,),
        in_specs=[PACKED],
        out_specs=FLAT,
        out_shape=jax.ShapeDtypeStruct((BLOCK, 2 * PLACES * HDIM), x.dtype),
    )(x)


def attention_kernel(
    first, last, parts, most, table_hbm, q_ref, *rest
):
    rest = list(rest)
    kv_hbm = [rest.pop(0) for _ in range(parts)]
    if not first:
        acc_in, top_in, total_in = (rest.pop(0) for _ in range(3))
    if last:
        o_ref = rest.pop(0)
        acc_ref, top_ref, total_ref = rest[5:8]
    else:
        acc_ref, top_ref, total_ref = (rest.pop(0) for _ in range(3))
    s0, s1, p0, p1, kv_ref = rest[:5]
    table, sems = rest[-2:]
    nq = q_ref.shape[0]

    copies = [(table_hbm, table)]
    at = 0
    for part in kv_hbm:
        copies.append((part, kv_ref.at[pl.ds(at, part.shape[0])]))
        at += part.shape[0]
    copies = [
        pltpu.make_async_copy(src, dst, sems.at[i]) for i, (src, dst) in enumerate(copies)
    ]
    for copy in copies:
        copy.start()
    if first:
        acc_ref[...] = jnp.zeros_like(acc_ref)
        top_ref[...] = jnp.full_like(top_ref, -jnp.inf)
        total_ref[...] = jnp.zeros_like(total_ref)
    else:
        acc_ref[...] = acc_in[...]
        top_ref[...] = top_in[...]
        total_ref[...] = total_in[...]
    for copy in copies:
        copy.wait()

    def where(t):
        code = table[t + (nq + 1) * (most + 1) + 1]
        return code // 16, code % 16

    def places(b, c):
        end = jnp.maximum(table[b] - 1, 0)
        return [table[(nq + 1) + b * most + jnp.minimum(c * GROUP + g, end)] for g in range(GROUP)]

    def scores(b, chosen, dst):
        rows = jnp.concatenate([kv_ref[i, 0] for i in chosen], axis=0)
        q = q_ref[jnp.minimum(b, nq - 1)]
        s = lax.dot_general(rows, q, (((1,), (1,)), ((), ())), preferred_element_type=jnp.float32)
        dst[...] = s
        return jnp.max(s.reshape(GROUP * BLOCK // 8, 8, BLOCK), axis=0)

    def weights(b, c, largest, src, dst, top, total):
        count = table[b]
        top = jnp.where(c == 0, top_ref[b], top)
        total = jnp.where(c == 0, total_ref[b], total)
        new_top = jnp.maximum(top, jnp.max(largest, axis=0, keepdims=True))
        shrink = jnp.exp2((top - new_top) * FACTOR)
        total = total * shrink
        for g in range(GROUP):
            rows = slice(g * BLOCK, (g + 1) * BLOCK)
            base = jnp.where(c * GROUP + g < count, new_top, jnp.inf)
            weight = jnp.exp2((src[rows, :] - base) * FACTOR)
            total = total + jnp.sum(weight.reshape(BLOCK // 8, 8, BLOCK), axis=0)
            dst[rows, :] = weight.astype(jnp.bfloat16)
        top_ref[b] = new_top
        total_ref[b] = total
        return new_top, total, shrink

    def weighted(b, chosen, shrink, src):
        cols = jnp.concatenate([kv_ref[i, 1] for i in chosen], axis=1)
        acc_ref[b] = acc_ref[b] * shrink + jnp.dot(
            cols, src[...], preferred_element_type=jnp.float32
        )

    steps = table[(nq + 1) * (most + 1)]
    score_bufs, weight_bufs = (s0, s1), (p0, p1)
    b0, c0 = where(0)
    places0 = places(b0, c0)
    largest0 = scores(b0, places0, s0)
    b1, c1 = where(1)
    places1 = places(b1, c1)
    largest1 = scores(b1, places1, s1)
    top, total, shrink0 = weights(
        b0,
        c0,
        largest0,
        s0,
        p0,
        jnp.full((1, BLOCK), -jnp.inf, jnp.float32),
        jnp.zeros((8, BLOCK), jnp.float32),
    )

    def body(start, unroll):
        def run(i, carry):
            b0, shrink0, b1, c1, largest1, top, total = carry[:7]
            places0, places1 = list(carry[7 : 7 + GROUP]), list(carry[7 + GROUP :])
            for u in range(unroll):
                b2, c2 = where(start + unroll * i + u + 2)
                places2 = places(b2, c2)
                largest2 = scores(b2, places2, score_bufs[u % 2])
                top, total, shrink1 = weights(
                    b1, c1, largest1, score_bufs[1 - u % 2], weight_bufs[1 - u % 2], top, total
                )
                weighted(b0, places0, shrink0, weight_bufs[u % 2])
                b0, shrink0, places0 = b1, shrink1, places1
                b1, c1, largest1, places1 = b2, c2, largest2, places2
            return (b0, shrink0, b1, c1, largest1, top, total, *places0, *places1)

        return run

    state = (b0, shrink0, b1, c1, largest1, top, total, *places0, *places1)
    done = 0
    for unroll in UNROLLS:
        extra = 1 if unroll == UNROLLS[-1] else 0
        rounds = (steps - done + extra) // unroll
        state = lax.fori_loop(0, rounds, body(done, unroll), state)
        done = done + rounds * unroll

    if last:

        def finish(b, _):
            out = acc_ref[b] * (1.0 / jnp.sum(total_ref[b], axis=0, keepdims=True))
            o_ref[b] = out.T.astype(jnp.bfloat16)
            return 0

        lax.fori_loop(0, nq, finish, 0, unroll=8)


def attention(table, most, q, kv, state, last):
    nq = q.shape[0]
    first = state is None
    hbm = pl.BlockSpec(memory_space=pl.ANY)
    shapes = [(nq + 1, HDIM, BLOCK), (nq + 1, 1, BLOCK), (nq + 1, 8, BLOCK)]
    vmem = pl.BlockSpec(memory_space=pltpu.VMEM)
    scratch = [
        pltpu.VMEM((GROUP * BLOCK, BLOCK), jnp.float32),
        pltpu.VMEM((GROUP * BLOCK, BLOCK), jnp.float32),
        pltpu.VMEM((GROUP * BLOCK, BLOCK), jnp.bfloat16),
        pltpu.VMEM((GROUP * BLOCK, BLOCK), jnp.bfloat16),
        pltpu.VMEM((sum(a.shape[0] for a in kv),) + kv[0].shape[1:], kv[0].dtype),
    ]
    if last:
        scratch += [pltpu.VMEM(s, jnp.float32) for s in shapes]
        out_shape = jax.ShapeDtypeStruct(q.shape, jnp.bfloat16)
        out_specs = vmem
    else:
        out_shape = [jax.ShapeDtypeStruct(s, jnp.float32) for s in shapes]
        out_specs = [vmem for s in shapes]
    scratch += [pltpu.SMEM(table.shape, jnp.int32), pltpu.SemaphoreType.DMA((len(kv) + 1,))]
    args = [q, *kv] + ([] if first else list(state))
    return pl.pallas_call(
        functools.partial(attention_kernel, first, last, len(kv), most),
        in_specs=[hbm, vmem] + [hbm] * len(kv) + [vmem] * (len(args) - 1 - len(kv)),
        out_specs=out_specs,
        scratch_shapes=scratch,
        out_shape=out_shape,
        compiler_params=pltpu.CompilerParams(vmem_limit_bytes=VMEM),
        cost_estimate=pl.CostEstimate(flops=1_000_000, bytes_accessed=1, transcendentals=0),
    )(table, *args)


def make_table(match, place):
    nq, most = match.shape
    at = jnp.arange(most, dtype=jnp.int32)
    before = (at[:, None] < at[None, :])[None] & match[:, :, None]
    pos = jnp.sum(before.astype(jnp.int32), axis=1)
    hit = (pos[:, :, None] == at[None, None, :]) & match[:, :, None]
    lists = jnp.sum(jnp.where(hit, place[:, :, None], 0), axis=1)
    counts = jnp.sum(match.astype(jnp.int32), axis=1)
    steps = (counts + GROUP - 1) // GROUP
    row = jnp.arange(nq, dtype=jnp.int32)
    ends = jnp.sum(jnp.where(row[:, None] <= row[None, :], steps[:, None], 0), axis=0)
    t = jnp.arange(nq * ((most + GROUP - 1) // GROUP) + 4, dtype=jnp.int32)
    b = jnp.sum((t[:, None] >= ends[None, :]).astype(jnp.int32), axis=1)
    start = jnp.sum(jnp.where(row[None, :] < b[:, None], steps[None, :], 0), axis=1)
    c = jnp.where(b < nq, t - start, 0)
    lists = jnp.pad(lists, ((0, 1), (0, 0))).reshape(-1)
    table = jnp.concatenate([jnp.pad(counts, (0, 1)), lists, ends[-1:], b * 16 + c])
    return jnp.pad(table, (0, -table.shape[0] % 1024))


def local(queries, keys, values, key_blocks, key_count):
    seq_count, head_count = lax.axis_size("seq"), lax.axis_size("head")
    y = lax.axis_index("head")
    core = lax.axis_index("seq") % 2

    index = lambda place, c, yy: (place * 2 + c) * head_count + yy
    groups = [
        [index(place, c, yy) for yy in ys for place in range(PLACES)]
        for c in range(2)
        for ys in ((0, 3), (1, 2))
    ]
    swap = lambda a: lax.all_to_all(
        a, ("seq", "head"), 0, 0, axis_index_groups=groups, tiled=True
    )
    to_core = lambda a: lax.ppermute(a, "seq", [(i, i ^ 1) for i in range(seq_count)])
    to_pair = lambda a: lax.ppermute(a, "head", [(i, i ^ 1) for i in range(head_count)])

    kv = pack_kv(keys, values)
    kv, key_blocks, key_count = lax.optimization_barrier((kv, key_blocks, key_count))

    odd = (y >= 2).astype(jnp.int32)
    mine = jnp.concatenate([key_blocks[0], key_count[0][:, None]], axis=1)
    mine = jnp.where(core == odd, mine, to_core(mine))
    outer = (y == 0) | (y == 3)
    mine = mine.reshape(head_count, PLACES, 2, -1)
    mine = lax.dynamic_index_in_dim(mine, core, 2, keepdims=False)
    mine = jnp.where(outer, mine[0::3], mine[1:3]).reshape(2 * PLACES, -1)
    blocks, count = mine[:, :-1], mine[:, -1]
    active = jnp.arange(blocks.shape[1], dtype=jnp.int32)[None, :] < count[:, None]
    block_y = blocks // 32
    block_core = (blocks % 2) ^ core
    block_place = (blocks // 2) % PLACES
    near = ((block_y == 0) | (block_y == 3)) == outer
    block_at = (block_y // 2) * PLACES + block_place
    size, most = 2 * PLACES, blocks.shape[1]
    early = near | (block_at < CUT)
    early_place = jnp.where(
        near, block_core * size + block_at, 2 * size + block_core * CUT + block_at
    )
    late_place = block_core * (size - CUT) + block_at - CUT
    early_table = make_table(active & early, early_place)
    late_table = make_table(active & ~early, late_place)

    kv, q, early_table, late_table = lax.optimization_barrier(
        (
            swap(kv.reshape(2 * PLACES, 2, BLOCK, HDIM)),
            pack_q(queries),
            early_table,
            late_table,
        )
    )
    far, far_late = kv[:CUT], kv[CUT:]
    kv, far_late = lax.optimization_barrier((kv, far_late))
    far, far_late = to_pair(far), to_pair(far_late)
    q = swap(q.reshape(2 * PLACES, BLOCK, HDIM))
    state = attention(early_table, most, q, [kv, to_core(kv), far, to_core(far)], None, False)
    state, far_late = lax.optimization_barrier((state, far_late))
    out = attention(late_table, most, q, [far_late, to_core(far_late)], state, True)
    return unpack(swap(out).reshape(2, PLACES, BLOCK, HDIM))


def solution(mesh):
    placed = (
        P(("head", "seq"), None),
        P(("head", "seq"), None),
        P(("head", "seq"), None),
        P("seq", None, None),
        P("seq", None),
    )
    return jax.shard_map(
        local, mesh=mesh, in_specs=placed, out_specs=P(("head", "seq"), None), check_vma=False
    )
```
